256 devices in a mesh: dp: 16 (over y, x), tensor: 16 (over z, core).
Axes of the slice: x: 4, y: 4, z: 8, core: 2. Of those that a mesh axis runs over, the one named last changes fastest.
Arguments:
- grad_up: bfloat16 [32768, 28672], P('dp', 'tensor'), may hold values from -240 to 240
- activations: bfloat16 [32768, 8192], P('dp', 'tensor'), may hold values from -6 to 6
- segment_ids: int32 [16, 2048], P('dp'), may hold values from 0 to 15, never falling along the last dimension, each value on 1 to 256 neighbouring positions
- proj_out: bfloat16 [64, 28672], P(None, 'tensor'), may hold values from -0.09449112 to 0.09449112
- proj_in: bfloat16 [64, 8192], P(None, 'tensor'), may hold values from -0.0625 to 0.0625
Outputs:
- fisher: float32 [4096, 4096], P('tensor', 'dp')
The draws below stay inside these ranges and needn't reach their ends.
Inputs may be any that keep to these rules, and one draw needn't show every extreme that they name: `segment_ids`: each row numbers its tokens' examples 0 to 15 in order, never falling; every example has 1 to 256 tokens, and one has exactly 256.
All inputs are finite; a program needn't handle non-finite values.
Results may differ from the reference program's by a relative error of at most 0.0003.
Values sent between devices are 32-bit elements; how exact they have to be, the bound alone decides.
A program may use at most 64 MiB of HBM per device.

```python
import math
import jax
import jax.numpy as jnp
import numpy as np
from jax import lax

D = 8192
FF = 28672
PROJ = 64
E_DEV = 16
TOK_DEV = 2048
MOST = 256
TOKENS = 32768
N_DP = 16


def draw_grad_up(key, part):
    key = jax.random.fold_in(key, 11)
    key_noise, key_scale = jax.random.split(key, 2)
    positions = jnp.arange(TOKENS, dtype=jnp.float32) / (TOKENS - 1)
    row_scale = jnp.exp(jax.random.uniform(key_scale, (TOKENS, 1), jnp.float32, 0.0, math.log(10.0)))
    noise = jnp.clip(jax.random.normal(key_noise, (TOKENS, FF), jnp.float32), -6.0, 6.0)
    ramp = 1.0 + positions
    return (noise * row_scale * ramp[:, None]).astype(jnp.bfloat16)


def draw_proj_out(key, part):
    key = jax.random.fold_in(key, 23)
    key_noise, key_scale = jax.random.split(key, 2)
    row_scale = jnp.exp(jax.random.uniform(key_scale, (PROJ, 1), jnp.float32, 0.0, math.log(10.0)))
    noise = jnp.clip(jax.random.normal(key_noise, (PROJ, FF), jnp.float32), -6.0, 6.0)
    return (noise * row_scale * (0.25 / math.sqrt(FF))).astype(jnp.bfloat16)


def block_scale(rng, dims, cuts, smallest, largest):
    factor_of, own = 1.0, jax.random.fold_in(rng, 6)
    for position, blocks in cuts:
        draws = jnp.exp(jax.random.uniform(jax.random.fold_in(own, position), (blocks,), jnp.float32, smallest / len(cuts), largest / len(cuts)))
        factor_of = factor_of * jnp.repeat(draws, dims[position] // blocks).reshape([-1 if axis == position else 1 for axis in range(len(dims))])
    return factor_of


def length_profile(count, total, reach, lean):
    loads = [(1 << 20) // math.isqrt(standing ** lean) + 1 for standing in range(2, count + 1)]
    spare, given = total - reach - (count - 1), [1] * (count - 1)
    while spare > 0:
        free = [i for i in range(count - 1) if given[i] < reach]
        mass, budget = sum([loads[i] for i in free]), spare
        for i in free:
            addition = min(reach - given[i], max(1, budget * loads[i] // mass), spare)
            given[i] = given[i] + addition
            spare = spare - addition
    return np.array([reach] + given)


def ragged(key, count, total, reach, skew):
    if count == 2:
        one = jax.random.randint(key, (), max(1, total - reach), min(reach, total - 1) + 1)
        return jnp.stack([one, total - one])
    lengths = jnp.asarray(length_profile(count, total, reach, skew), jnp.int32)
    twos = (count - 1) // 2
    giver, receiver = lengths[1:1 + 2 * twos:2], lengths[2:2 + 2 * twos:2]
    margin = jnp.minimum(giver - 1, reach - receiver)
    shifted = jax.random.randint(jax.random.fold_in(key, 1), (twos,), 0, 1 << 20) % (margin + 1)
    lengths = lengths.at[1:1 + 2 * twos:2].set(giver - shifted).at[2:2 + 2 * twos:2].set(receiver + shifted)
    return lengths[jax.random.permutation(jax.random.fold_in(key, 2), count)]


def centred(key, dims, deviation, limit, cuts=(), kind=jnp.bfloat16):
    result = jax.random.normal(key, dims, jnp.float32) * deviation
    if len(cuts) > 0:
        result = block_scale(key, dims, cuts, -0.22, 0.18) * result
    return jnp.clip(result, min=-limit, max=limit).astype(kind)


def setup_inputs(seed: int = 0) -> dict:
    arg_keys = jax.random.split(jax.random.key(seed), 6)
    return {
        "grad_up": draw_grad_up(jax.random.fold_in(arg_keys[5], 71), 0),
        "activations": centred(arg_keys[1], (TOKENS, D), 1.0, 6.0, ((0, 16), (1, 16))),
        "segment_ids": jax.vmap(lambda own: jnp.searchsorted(jnp.cumsum(ragged(own, E_DEV, TOK_DEV, MOST, 1)), jnp.arange(TOK_DEV), side="right"))(jax.random.split(arg_keys[2], N_DP)).reshape((N_DP, TOK_DEV)).astype(jnp.int32),
        "proj_out": draw_proj_out(jax.random.fold_in(arg_keys[5], 71), 0),
        "proj_in": centred(arg_keys[4], (PROJ, D), D ** -0.5, 0.0625, ((1, 16),)),
    }


def reference(grad_up, activations, segment_ids, proj_out, proj_in):
    grad_groups = grad_up.reshape(N_DP, TOK_DEV, FF)
    act_groups = activations.reshape(N_DP, TOK_DEV, D)

    def one_group(inputs):
        grad_rows, act_rows, segment_row = inputs
        out_proj = jnp.dot(grad_rows, proj_out.T, preferred_element_type=jnp.float32)
        in_proj = jnp.dot(act_rows, proj_in.T, preferred_element_type=jnp.float32)
        member = (segment_row[:, None] == jnp.arange(E_DEV, dtype=jnp.int32)[None, :]).astype(jnp.float32)
        outer = (out_proj[:, :, None] * in_proj[:, None, :]).reshape(TOK_DEV, PROJ * PROJ)
        return jnp.dot(member.T, outer, precision=lax.Precision.HIGHEST)

    per_example = lax.map(one_group, (grad_groups, act_groups, segment_ids)).reshape(N_DP * E_DEV, PROJ * PROJ)
    raw_fisher = jnp.dot(per_example.T, per_example, precision=lax.Precision.HIGHEST)
    trace = jnp.sum(per_example * per_example)
    return raw_fisher / (trace / (PROJ * PROJ) + 1e-6)
```

```python
import functools

import jax
import jax.numpy as jnp
from jax import lax
from jax.experimental import pallas as pl
from jax.experimental.pallas import tpu as pltpu
from jax.sharding import PartitionSpec as P

MESH = pl.DeviceIdType.MESH
F32 = jnp.float32
BF16 = jnp.bfloat16
EXAMPLES = 16
PROJ = 64
LANES = 128


def split(x):
    high = x.astype(BF16)
    low = (x - high.astype(F32)).astype(BF16)
    return high, low


def order(i):
    return 4 - (i + 1) // 2 if i % 2 else 4 + i // 2


def kernel(
    ndp, nz, nt,
    grad_hbm, act_hbm, seg_hbm, po_hbm, pi_hbm, out_ref,
    gbuf, abuf, seg, wout, win, part, sib_recv, rs_send, rs_recv, tok,
    high_ref, low_ref, xacc, xs_recv, xd, msg, rows, cols, ss, ss_recv,
    g_sem, a_sem, w_sem, sib_s, sib_r, rs_s, rs_r, ag_s, ag_r, xs_sem,
    row_s, row_r, col_s, col_r, fw_s, fw_r, ss_sem,
):
    d = lax.axis_index("dp")
    t = lax.axis_index("tensor")
    z, c = t // 2, t % 2
    sibling = (d, t + 1 - 2 * c)
    chunk = 2 * nt

    def zdev(k):
        return (d, ((z + k) % nz) * 2 + c)

    def remote(src, dst, send, recv, device):
        return pltpu.make_async_remote_copy(
            src_ref=src, dst_ref=dst, send_sem=send, recv_sem=recv,
            device_id=device, device_id_type=MESH,
        )

    barrier = pltpu.get_barrier_semaphore()
    for k in range(1, nz):
        pl.semaphore_signal(barrier, inc=1, device_id=zdev(k), device_id_type=MESH)
    for k in range(1, ndp):
        pl.semaphore_signal(barrier, inc=1, device_id=((d + k) % ndp, t), device_id_type=MESH)
    pl.semaphore_signal(barrier, inc=1, device_id=sibling, device_id_type=MESH)

    weights = [
        pltpu.make_async_copy(po_hbm, wout.at[pl.ds(0, PROJ)], w_sem.at[0]),
        pltpu.make_async_copy(pi_hbm, win.at[pl.ds(PROJ, PROJ)], w_sem.at[1]),
        pltpu.make_async_copy(seg_hbm, seg, w_sem.at[2]),
    ]
    for copy in weights:
        copy.start()
    loads = []
    for i in range(nz):
        first = pl.multiple_of(((z + order(i)) % nz) * chunk, chunk)
        loads.append((
            pltpu.make_async_copy(grad_hbm.at[pl.ds(first, chunk)], gbuf.at[i], g_sem.at[i]),
            pltpu.make_async_copy(act_hbm.at[pl.ds(first, chunk)], abuf.at[i], a_sem.at[i]),
        ))
        loads[-1][0].start()
        loads[-1][1].start()

    wout[pl.ds(PROJ, PROJ)] = jnp.zeros((PROJ, wout.shape[1]), BF16)
    win[pl.ds(0, PROJ)] = jnp.zeros((PROJ, win.shape[1]), BF16)
    xacc[...] = jnp.zeros_like(xacc)
    for copy in weights:
        copy.wait()

    last = (((1,), (1,)), ((), ()))
    for i in range(nz):
        loads[i][0].wait()
        loads[i][1].wait()
        summed = lax.dot_general(gbuf[i], wout[...], last, preferred_element_type=F32)
        summed += lax.dot_general(abuf[i], win[...], last, preferred_element_type=F32)
        part[i] = summed.reshape(2, nt, LANES)

    pl.semaphore_wait(barrier, nz - 1 + ndp - 1 + 1)

    sib = [
        remote(part.at[i, 1 - c], sib_recv.at[i], sib_s.at[i], sib_r.at[i], sibling)
        for i in range(nz)
    ]
    for copy in sib:
        copy.start()
    scatter = [
        remote(rs_send.at[i], rs_recv.at[i], rs_s.at[i], rs_r.at[i], zdev(order(i)))
        for i in range(nz - 1)
    ]
    for i in range(nz):
        sib[i].wait_recv()
        rs_send[i] = part[i, c] + sib_recv[i]
        if i < nz - 1:
            scatter[i].start()
    total = rs_send[nz - 1]
    for i in range(nz - 1):
        scatter[i].wait_recv()
        total += rs_recv[i]
    tok[z] = total
    gather = [
        remote(tok.at[z], tok.at[z], ag_s.at[i], ag_r.at[z], zdev(order(i)))
        for i in range(nz - 1)
    ]
    for copy in gather:
        copy.start()

    lane = lax.broadcasted_iota(jnp.int32, (nt, LANES), 1)
    example = lax.broadcasted_iota(jnp.int32, (EXAMPLES, nt), 0)

    def accumulate(owner):
        sums = tok[owner]
        flipped = sums.T
        high = flipped[:PROJ].astype(BF16).astype(F32)
        high_ref[...] = high
        low_ref[...] = flipped[:PROJ] - high
        first = pl.multiple_of(owner * chunk + c * nt, nt)
        member = seg[:, pl.ds(first, nt)] == example
        even = jnp.where(lane < PROJ, pltpu.roll(sums, PROJ, 1), 0.0)
        odd = jnp.where(lane < PROJ, 0.0, sums)
        in_high, in_low = split(jnp.concatenate([even, odd], axis=0))
        both = jnp.concatenate([in_high, in_low], axis=1)

        def weigh(ref, p):
            pair = [
                jnp.where(member, jnp.broadcast_to(ref[pl.ds(p + parity, 1), :], member.shape), 0.0)
                for parity in range(2)
            ]
            return jnp.concatenate(pair, axis=1).astype(BF16)

        for half in range(2):
            for quarter in range(4):
                ps = [
                    8 * zz + 4 * half + 2 * jj
                    for zz in (2 * quarter, 2 * quarter + 1) for jj in range(2)
                ]
                w_high = jnp.concatenate([weigh(high_ref, p) for p in ps], axis=0)
                w_low = jnp.concatenate([weigh(low_ref, p) for p in ps], axis=0)
                one = jnp.dot(w_high, both, preferred_element_type=F32)
                two = jnp.dot(w_low, in_high, preferred_element_type=F32)
                block = one[:, :LANES] + (one[:, LANES:] + two)
                xacc[half, pl.ds(2 * quarter, 2)] += block.reshape(2, 2 * EXAMPLES, LANES)

    accumulate(z)
    for i in range(nz - 1):
        owner = (z - order(i) + nz) % nz
        remote(tok.at[z], tok.at[owner], ag_s.at[i], ag_r.at[owner], zdev(order(i))).wait_recv()
        accumulate(owner)

    swap = remote(xacc.at[1 - c], xs_recv, xs_sem.at[0], xs_sem.at[1], sibling)
    swap.start()
    swap.wait_recv()
    mine = xacc[c] + xs_recv[...]
    xd[...] = mine
    msg[pl.ds(0, 2 * EXAMPLES)] = xd[z]
    msg[pl.ds(2 * EXAMPLES, 8)] = jnp.sum((mine * mine).reshape(-1, 8, LANES), axis=0)

    home = d // 2
    forwards = c == d % 2

    def column(m):
        place = (home + m) % (ndp // 2)
        return remote(
            xd.at[place], cols.at[d], col_s.at[m], col_r.at[d], (2 * place + c, t)
        )

    def column_from(source):
        return remote(xd.at[0], cols.at[source], col_s.at[0], col_r.at[source], (source, t))

    def forward(source):
        return remote(cols.at[source], cols.at[source], fw_s.at[source], fw_r.at[source], sibling)

    def row(k):
        return remote(msg, rows.at[d], row_s.at[k], row_r.at[d], ((d + k) % ndp, t))

    def row_from(source):
        return remote(msg, rows.at[source], row_s.at[1], row_r.at[source], (source, t))

    for m in range(1, ndp // 2):
        column(m).start()

    @pl.when(jnp.logical_not(forwards))
    def _():
        column(0).start()

    for k in range(1, ndp):
        row(k).start()
    rows[d] = msg[...]

    @pl.when(forwards)
    def _():
        cols[d] = xd[home]
        forward(d).start()
        for k in range(1, ndp):
            source = (d + k) % ndp
            column_from(source).wait_recv()
            forward(source).start()

    for k in range(1, ndp):
        row_from((d + k) % ndp).wait_recv()
    ss[...] = jnp.sum(rows[:, pl.ds(2 * EXAMPLES, 8), :], axis=0)
    swap_ss = remote(ss, ss_recv, ss_sem.at[0], ss_sem.at[1], sibling)
    swap_ss.start()

    def matrix(ref):
        return jnp.concatenate(
            [
                ref[:, pl.ds(jj * EXAMPLES, EXAMPLES), :].reshape(ndp * EXAMPLES, LANES)
                for jj in range(2)
            ],
            axis=1,
        )

    left_high, left_low = split(matrix(rows).T)

    @pl.when(jnp.logical_not(forwards))
    def _():
        for k in range(ndp):
            forward((d + k) % ndp).wait_recv()

    right_high, right_low = split(matrix(cols))
    swap_ss.wait_recv()
    trace = jnp.sum(ss[...] + ss_recv[...])
    scale = 1.0 / (trace / (PROJ * PROJ) + 1e-6)
    raw = jnp.dot(left_high, right_high, preferred_element_type=F32)
    raw += jnp.dot(left_high, right_low, preferred_element_type=F32)
    raw += jnp.dot(left_low, right_high, preferred_element_type=F32)
    out_ref[...] = raw * scale

    for copy in sib + scatter + gather + [swap, swap_ss]:
        copy.wait_send()
    for m in range(1, ndp // 2):
        column(m).wait_send()
    for k in range(1, ndp):
        row(k).wait_send()

    @pl.when(forwards)
    def _():
        for k in range(ndp):
            forward(k).wait_send()

    @pl.when(jnp.logical_not(forwards))
    def _():
        column(0).wait_send()


def shards(ndp, nz, grad_up, activations, segment_ids, proj_out, proj_in):
    tokens, hidden = grad_up.shape
    features = activations.shape[1]
    nt = tokens // (2 * nz)
    rows = 2 * EXAMPLES
    dma = pltpu.SemaphoreType.DMA
    return pl.pallas_call(
        functools.partial(kernel, ndp, nz, nt),
        out_shape=jax.ShapeDtypeStruct((4 * PROJ, 4 * PROJ), F32),
        in_specs=[pl.BlockSpec(memory_space=pl.ANY)] * 5,
        out_specs=pl.BlockSpec(memory_space=pltpu.VMEM),
        scratch_shapes=[
            pltpu.VMEM((nz, 2 * nt, hidden), BF16),
            pltpu.VMEM((nz, 2 * nt, features), BF16),
            pltpu.VMEM((1, tokens), jnp.int32),
            pltpu.VMEM((2 * PROJ, hidden), BF16),
            pltpu.VMEM((2 * PROJ, features), BF16),
            pltpu.VMEM((nz, 2, nt, LANES), F32),
            pltpu.VMEM((nz, nt, LANES), F32),
            pltpu.VMEM((nz, nt, LANES), F32),
            pltpu.VMEM((nz, nt, LANES), F32),
            pltpu.VMEM((nz, nt, LANES), F32),
            pltpu.VMEM((PROJ, nt), F32),
            pltpu.VMEM((PROJ, nt), F32),
            pltpu.VMEM((2, nz, rows, LANES), F32),
            pltpu.VMEM((nz, rows, LANES), F32),
            pltpu.VMEM((nz, rows, LANES), F32),
            pltpu.VMEM((rows + 8, LANES), F32),
            pltpu.VMEM((ndp, rows + 8, LANES), F32),
            pltpu.VMEM((ndp, rows, LANES), F32),
            pltpu.VMEM((8, LANES), F32),
            pltpu.VMEM((8, LANES), F32),
            dma((nz,)), dma((nz,)), dma((3,)),
            dma((nz,)), dma((nz,)), dma((nz,)), dma((nz,)), dma((nz,)), dma((nz,)), dma((2,)),
            dma((ndp,)), dma((ndp,)), dma((ndp,)), dma((ndp,)), dma((ndp,)), dma((ndp,)), dma((2,)),
        ],
        compiler_params=pltpu.CompilerParams(
            collective_id=0, has_side_effects=True, vmem_limit_bytes=56 * 2**20
        ),
        cost_estimate=pl.CostEstimate(
            flops=2 * tokens * (hidden + features) * PROJ,
            bytes_accessed=2 * tokens * (hidden + features),
            transcendentals=0,
        ),
    )(grad_up, activations, segment_ids, proj_out, proj_in)


def solution(mesh):
    in_specs = (
        P("dp", "tensor"),
        P("dp", "tensor"),
        P("dp", None),
        P(None, "tensor"),
        P(None, "tensor"),
    )
    body = functools.partial(shards, mesh.shape["dp"], mesh.shape["tensor"] // 2)
    return jax.shard_map(
        body, mesh=mesh, in_specs=in_specs, out_specs=P("tensor", "dp"), check_vma=False
    )
```

```python
import functools

import jax
import jax.numpy as jnp
from jax import lax
from jax.experimental import pallas as pl
from jax.experimental.pallas import tpu as pltpu
from jax.sharding import PartitionSpec as P

MESH = pl.DeviceIdType.MESH
F32 = jnp.float32
BF16 = jnp.bfloat16
EXAMPLES = 16
PROJ = 64
LANES = 128


def split(x):
    high = x.astype(BF16)
    low = (x - high.astype(F32)).astype(BF16)
    return high, low


def order(i):
    return 4 - (i + 1) // 2 if i % 2 else 4 + i // 2


def kernel(
    ndp, nz, nt,
    grad_hbm, act_hbm, seg_hbm, po_hbm, pi_hbm, left_ref, right_ref, scale_ref,
    gbuf, abuf, seg, wout, win, wt_out, wt_in, part, sib_recv, sums, far_recv, near_recv, tok,
    high_ref, low_ref, xacc, xs_recv, xd, msg, rows, cols, ss, ss_recv,
    g_sem, a_sem, w_sem, sib_s, sib_r, far_s, far_r, near_s, near_r, ag_s, ag_r, fa_s, fa_r,
    xs_sem, row_s, row_r, col_s, col_r, fw_s, fw_r, ss_sem,
):
    d = lax.axis_index("dp")
    t = lax.axis_index("tensor")
    z, c = t // 2, t % 2
    sibling = (d, t + 1 - 2 * c)
    chunk = 2 * nt

    def zdev(k):
        return (d, ((z + k + nz) % nz) * 2 + c)

    def remote(src, dst, send, recv, device):
        return pltpu.make_async_remote_copy(
            src_ref=src, dst_ref=dst, send_sem=send, recv_sem=recv,
            device_id=device, device_id_type=MESH,
        )

    barrier = pltpu.get_barrier_semaphore()
    for k in (1, -1, 2, -2):
        pl.semaphore_signal(barrier, inc=1, device_id=zdev(k), device_id_type=MESH)
    for k in range(1, ndp):
        pl.semaphore_signal(barrier, inc=1, device_id=((d + k) % ndp, t), device_id_type=MESH)
    pl.semaphore_signal(barrier, inc=1, device_id=sibling, device_id_type=MESH)

    weights = [
        pltpu.make_async_copy(po_hbm, wout.at[pl.ds(0, PROJ)], w_sem.at[0]),
        pltpu.make_async_copy(pi_hbm, win.at[pl.ds(PROJ, PROJ)], w_sem.at[1]),
        pltpu.make_async_copy(seg_hbm, seg, w_sem.at[2]),
    ]
    for copy in weights:
        copy.start()
    loads = []
    for i in range(nz):
        first = pl.multiple_of(((z + order(i)) % nz) * chunk, chunk)
        loads.append((
            pltpu.make_async_copy(grad_hbm.at[pl.ds(first, chunk)], gbuf.at[i], g_sem.at[i]),
            pltpu.make_async_copy(act_hbm.at[pl.ds(first, chunk)], abuf.at[i], a_sem.at[i]),
        ))
        loads[-1][0].start()
        loads[-1][1].start()

    wout[pl.ds(PROJ, PROJ)] = jnp.zeros((PROJ, wout.shape[1]), BF16)
    win[pl.ds(0, PROJ)] = jnp.zeros((PROJ, win.shape[1]), BF16)
    xacc[...] = jnp.zeros_like(xacc)
    for copy in weights:
        copy.wait()
    wt_out[...] = wout[...].T
    wt_in[...] = win[...].T

    def project(i):
        loads[i][0].wait()
        loads[i][1].wait()
        for h in range(2):
            at = pl.ds(h * nt, nt)
            both = jnp.dot(gbuf[i, at], wt_out[...], preferred_element_type=F32)
            both += jnp.dot(abuf[i, at], wt_in[...], preferred_element_type=F32)
            part[i, h] = both.reshape(2, nt // 2, LANES)

    ahead = 3
    for i in range(ahead):
        project(i)
    pl.semaphore_wait(barrier, 4 + ndp - 1 + 1)

    sib = [
        remote(part.at[i, 1 - c], sib_recv.at[i], sib_s.at[i], sib_r.at[i], sibling)
        for i in range(nz)
    ]
    at = {order(i) - nz if order(i) > 4 else order(i): i for i in range(nz)}
    sides = (1, -1)

    def far(s, h):
        n = 2 * s + h
        return remote(
            sums.at[at[3 * sides[s]], h], far_recv.at[s, h], far_s.at[n], far_r.at[n], zdev(sides[s])
        )

    def farthest(s):
        return remote(
            sums.at[at[4], s], far_recv.at[2, s], far_s.at[4 + s], far_r.at[4 + s], zdev(2 * sides[s])
        )

    def near(s):
        return remote(sums.at[at[sides[s]]], near_recv.at[s], near_s.at[s], near_r.at[s], zdev(sides[s]))

    def second(s, h):
        n = 2 + 2 * s + h
        return remote(
            sums.at[at[2 * sides[s]], h], near_recv.at[2 + s, h], near_s.at[n], near_r.at[n],
            zdev(2 * sides[s]),
        )

    for i in range(ahead):
        sib[i].start()
    for i in range(nz):
        if i + ahead < nz:
            project(i + ahead)
            sib[i + ahead].start()
        sib[i].wait_recv()
        sums[i] = part[i, c] + sib_recv[i]
        if i == at[4]:
            farthest(0).start()
            farthest(1).start()
        for s in range(2):
            if i == at[3 * sides[s]]:
                far(s, 1 - s).start()
                far(s, s).start()
            if i == at[sides[s]]:
                near(s).start()
    for s in range(2):
        far(s, 1 - s).wait_recv()
        sums[at[2 * sides[s]], 1 - s] += far_recv[s, 1 - s]
        second(s, 1 - s).start()
    for s in range(2):
        far(s, s).wait_recv()
        farthest(s).wait_recv()
        sums[at[2 * sides[s]], s] += far_recv[s, s] + far_recv[2, s]
        second(s, s).start()
    for s in range(2):
        near(s).wait_recv()
    tok[z] = sums[at[0]] + (near_recv[0] + near_recv[1])
    for h in range(2):
        second(0, h).wait_recv()
        second(1, h).wait_recv()
        tok[z, h] += near_recv[2, h] + near_recv[3, h]

    def owner(k):
        return (z + k + nz) % nz

    def spread(s, h):
        n = 2 * s + h
        return remote(tok.at[z, h], tok.at[z, h], ag_s.at[n], ag_r.at[n], zdev(2 * sides[s]))

    def beside(s):
        return remote(tok.at[z], tok.at[z], ag_s.at[4 + s], ag_r.at[4 + s], zdev(sides[s]))

    def onward(s, h):
        n = 2 * s + h
        mine = tok.at[owner(-2 * sides[s]), h]
        return remote(mine, mine, fa_s.at[n], fa_r.at[n], zdev(sides[s]))

    def opposite(s):
        mine = tok.at[owner(-2 * sides[s]), s]
        return remote(mine, mine, fa_s.at[4 + s], fa_r.at[4 + s], zdev(2 * sides[s]))

    for first in range(2):
        for s in range(2):
            spread(s, s if first == 0 else 1 - s).start()
    for s in range(2):
        beside(s).start()

    lane = lax.broadcasted_iota(jnp.int32, (nt, LANES), 1)
    example = lax.broadcasted_iota(jnp.int32, (EXAMPLES, nt), 0)

    def accumulate(chip):
        whole = tok[chip].reshape(nt, LANES)
        flipped = whole.T
        high = flipped[:PROJ].astype(BF16).astype(F32)
        high_ref[...] = high
        low_ref[...] = flipped[:PROJ] - high
        first = pl.multiple_of(chip * chunk + c * nt, nt)
        member = seg[:, pl.ds(first, nt)] == example
        even = jnp.where(lane < PROJ, pltpu.roll(whole, PROJ, 1), 0.0)
        odd = jnp.where(lane < PROJ, 0.0, whole)
        in_high, in_low = split(jnp.concatenate([even, odd], axis=0))
        both = jnp.concatenate([in_high, in_low], axis=1)

        def weigh(ref, p):
            pair = [
                jnp.where(member, jnp.broadcast_to(ref[pl.ds(p + parity, 1), :], member.shape), 0.0)
                for parity in range(2)
            ]
            return jnp.concatenate(pair, axis=1).astype(BF16)

        for half in range(2):
            for quarter in range(4):
                ps = [
                    8 * zz + 4 * half + 2 * jj
                    for zz in (2 * quarter, 2 * quarter + 1) for jj in range(2)
                ]
                w_high = jnp.concatenate([weigh(high_ref, p) for p in ps], axis=0)
                w_low = jnp.concatenate([weigh(low_ref, p) for p in ps], axis=0)
                one = jnp.dot(w_high, both, preferred_element_type=F32)
                two = jnp.dot(w_low, in_high, preferred_element_type=F32)
                block = one[:, :LANES] + (one[:, LANES:] + two)
                xacc[half, pl.ds(2 * quarter, 2)] += block.reshape(2, 2 * EXAMPLES, LANES)

    accumulate(z)
    for s in range(2):
        spread(s, s).wait_recv()
        opposite(s).start()
        onward(s, s).start()
    for s in range(2):
        spread(s, 1 - s).wait_recv()
        onward(s, 1 - s).start()
    for s in range(2):
        accumulate(owner(-2 * sides[s]))
    for s in range(2):
        beside(s).wait_recv()
        accumulate(owner(-sides[s]))
    for s in range(2):
        for h in range(2):
            onward(s, h).wait_recv()
        accumulate(owner(-3 * sides[s]))
    for s in range(2):
        opposite(s).wait_recv()
    accumulate(owner(4))

    swap = remote(xacc.at[1 - c], xs_recv, xs_sem.at[0], xs_sem.at[1], sibling)
    swap.start()
    swap.wait_recv()
    mine = xacc[c] + xs_recv[...]
    xd[...] = mine
    msg[pl.ds(0, 2 * EXAMPLES)] = xd[z]
    msg[pl.ds(2 * EXAMPLES, 8)] = jnp.sum((mine * mine).reshape(-1, 8, LANES), axis=0)

    home = d // 2
    forwards = c == d % 2

    def column(m):
        place = (home + m) % (ndp // 2)
        return remote(
            xd.at[place], cols.at[d], col_s.at[m], col_r.at[d], (2 * place + c, t)
        )

    def column_from(source):
        return remote(xd.at[0], cols.at[source], col_s.at[0], col_r.at[source], (source, t))

    def forward(source):
        return remote(cols.at[source], cols.at[source], fw_s.at[source], fw_r.at[source], sibling)

    def row(k):
        return remote(msg, rows.at[d], row_s.at[k], row_r.at[d], ((d + k) % ndp, t))

    def row_from(source):
        return remote(msg, rows.at[source], row_s.at[1], row_r.at[source], (source, t))

    for m in range(1, ndp // 2):
        column(m).start()

    @pl.when(jnp.logical_not(forwards))
    def _():
        column(0).start()

    for k in range(1, ndp):
        row(k).start()
    rows[d] = msg[...]

    @pl.when(forwards)
    def _():
        cols[d] = xd[home]
        forward(d).start()
        for k in range(1, ndp):
            source = (d + k) % ndp
            column_from(source).wait_recv()
            forward(source).start()

    for k in range(1, ndp):
        row_from((d + k) % ndp).wait_recv()
    ss[...] = jnp.sum(rows[:, pl.ds(2 * EXAMPLES, 8), :], axis=0)
    swap_ss = remote(ss, ss_recv, ss_sem.at[0], ss_sem.at[1], sibling)
    swap_ss.start()

    def matrix(ref, out):
        for jj in range(2):
            out[:, pl.ds(jj * LANES, LANES)] = ref[:, pl.ds(jj * EXAMPLES, EXAMPLES), :].reshape(
                ndp * EXAMPLES, LANES
            )

    matrix(rows, left_ref)

    @pl.when(jnp.logical_not(forwards))
    def _():
        for k in range(ndp):
            forward((d + k) % ndp).wait_recv()

    matrix(cols, right_ref)
    swap_ss.wait_recv()
    trace = jnp.sum(ss[...] + ss_recv[...], keepdims=True)
    scale_ref[...] = trace / (PROJ * PROJ) + 1e-6

    for copy in sib + [swap, swap_ss]:
        copy.wait_send()
    for s in range(2):
        for copy in (farthest(s), near(s), beside(s), opposite(s)):
            copy.wait_send()
        for h in range(2):
            for copy in (far(s, h), second(s, h), spread(s, h), onward(s, h)):
                copy.wait_send()
    for m in range(1, ndp // 2):
        column(m).wait_send()
    for k in range(1, ndp):
        row(k).wait_send()

    @pl.when(forwards)
    def _():
        for k in range(ndp):
            forward(k).wait_send()

    @pl.when(jnp.logical_not(forwards))
    def _():
        column(0).wait_send()


def shards(ndp, nz, grad_up, activations, segment_ids, proj_out, proj_in):
    tokens, hidden = grad_up.shape
    features = activations.shape[1]
    nt = tokens // (2 * nz)
    rows = 2 * EXAMPLES
    block = 4 * PROJ
    dma = pltpu.SemaphoreType.DMA
    halves = (2, nt // 2, LANES)
    left, right, scale = pl.pallas_call(
        functools.partial(kernel, ndp, nz, nt),
        out_shape=[
            jax.ShapeDtypeStruct((ndp * EXAMPLES, block), F32),
            jax.ShapeDtypeStruct((ndp * EXAMPLES, block), F32),
            jax.ShapeDtypeStruct((1, 1), F32),
        ],
        in_specs=[pl.BlockSpec(memory_space=pl.ANY)] * 5,
        out_specs=[pl.BlockSpec(memory_space=pltpu.VMEM)] * 3,
        scratch_shapes=[
            pltpu.VMEM((nz, 2 * nt, hidden), BF16),
            pltpu.VMEM((nz, 2 * nt, features), BF16),
            pltpu.VMEM((1, tokens), jnp.int32),
            pltpu.VMEM((2 * PROJ, hidden), BF16),
            pltpu.VMEM((2 * PROJ, features), BF16),
            pltpu.VMEM((hidden, 2 * PROJ), BF16),
            pltpu.VMEM((features, 2 * PROJ), BF16),
            pltpu.VMEM((nz, 2) + halves, F32),
            pltpu.VMEM((nz,) + halves, F32),
            pltpu.VMEM((nz,) + halves, F32),
            pltpu.VMEM((3,) + halves, F32),
            pltpu.VMEM((4,) + halves, F32),
            pltpu.VMEM((nz,) + halves, F32),
            pltpu.VMEM((PROJ, nt), F32),
            pltpu.VMEM((PROJ, nt), F32),
            pltpu.VMEM((2, nz, rows, LANES), F32),
            pltpu.VMEM((nz, rows, LANES), F32),
            pltpu.VMEM((nz, rows, LANES), F32),
            pltpu.VMEM((rows + 8, LANES), F32),
            pltpu.VMEM((ndp, rows + 8, LANES), F32),
            pltpu.VMEM((ndp, rows, LANES), F32),
            pltpu.VMEM((8, LANES), F32),
            pltpu.VMEM((8, LANES), F32),
            dma((nz,)), dma((nz,)), dma((3,)),
            dma((nz,)), dma((nz,)), dma((6,)), dma((6,)), dma((6,)), dma((6,)),
            dma((6,)), dma((6,)), dma((6,)), dma((6,)), dma((2,)),
            dma((ndp,)), dma((ndp,)), dma((ndp,)), dma((ndp,)), dma((ndp,)), dma((ndp,)), dma((2,)),
        ],
        compiler_params=pltpu.CompilerParams(
            collective_id=0, has_side_effects=True, vmem_limit_bytes=56 * 2**20
        ),
        cost_estimate=pl.CostEstimate(
            flops=2 * tokens * (hidden + features) * PROJ,
            bytes_accessed=2 * tokens * (hidden + features),
            transcendentals=0,
        ),
    )(grad_up, activations, segment_ids, proj_out, proj_in)
    raw = lax.dot_general(
        left, right, (((0,), (0,)), ((), ())),
        precision=lax.Precision.HIGHEST, preferred_element_type=F32,
    )
    return raw / scale[0, 0]


def solution(mesh):
    in_specs = (
        P("dp", "tensor"),
        P("dp", "tensor"),
        P("dp", None),
        P(None, "tensor"),
        P(None, "tensor"),
    )
    body = functools.partial(shards, mesh.shape["dp"], mesh.shape["tensor"] // 2)
    return jax.shard_map(
        body, mesh=mesh, in_specs=in_specs, out_specs=P("tensor", "dp"), check_vma=False
    )
```

```python
import functools

import jax
import jax.numpy as jnp
from jax import lax
from jax.experimental import pallas as pl
from jax.experimental.pallas import tpu as pltpu
from jax.sharding import PartitionSpec as P

MESH = pl.DeviceIdType.MESH
F32 = jnp.float32
BF16 = jnp.bfloat16
EXAMPLES = 16
PROJ = 64
LANES = 128
DEPTH = 256
SIDE = 4


def split(x):
    high = x.astype(BF16)
    low = (x - high.astype(F32)).astype(BF16)
    return high, low


def order(i):
    return 4 - (i + 1) // 2 if i % 2 else 4 + i // 2


def kernel(
    ndp, nz, nt,
    grad_hbm, act_hbm, seg_hbm, po_hbm, pi_hbm, left_ref, right_ref, scale_ref,
    gbuf, abuf, seg, wout, win, wt_out, wt_in, part, sib_recv, sums, far_recv, near_recv, tok,
    high_ref, low_ref, xacc, rows, cols, ss, ss_all, ss_sum, ss_recv,
    g_sem, a_sem, w_sem, sib_s, sib_r, far_s, far_r, near_s, near_r, ag_s, ag_r, fa_s, fa_r,
    sh_s, sh_r, row_s, row_r, col_s, col_r, fw_s, fw_r, sq_s, sq_r, ss_sem, ready,
):
    d = lax.axis_index("dp")
    t = lax.axis_index("tensor")
    z, c = lax.div(t, 2), lax.rem(t, 2)
    ring = [lax.rem(z + k, nz) for k in range(nz)]
    plane = [lax.rem(d + k, ndp) for k in range(ndp)]
    sibling = (d, t + 1 - 2 * c)
    chunk = 2 * nt

    def zdev(k):
        return (d, ring[k % nz] * 2 + c)

    def remote(src, dst, send, recv, device):
        return pltpu.make_async_remote_copy(
            src_ref=src, dst_ref=dst, send_sem=send, recv_sem=recv,
            device_id=device, device_id_type=MESH,
        )

    barrier = pltpu.get_barrier_semaphore()
    line = [(lax.div(d, SIDE) * SIDE + lax.rem(d + k, SIDE), t) for k in range(1, SIDE)]
    column_peers = [(plane[SIDE * k], t) for k in range(1, ndp // SIDE)]
    greeted = [zdev(k) for k in (1, -1, 2, -2)] + line + column_peers + [sibling]
    for device in greeted:
        pl.semaphore_signal(barrier, inc=1, device_id=device, device_id_type=MESH)

    weights = [
        pltpu.make_async_copy(po_hbm, wout.at[pl.ds(0, PROJ)], w_sem.at[0]),
        pltpu.make_async_copy(pi_hbm, win.at[pl.ds(PROJ, PROJ)], w_sem.at[1]),
        pltpu.make_async_copy(seg_hbm, seg, w_sem.at[2]),
    ]
    for copy in weights:
        copy.start()
    loads = []
    for i in range(nz):
        first = pl.multiple_of(ring[order(i)] * chunk, chunk)
        loads.append((
            pltpu.make_async_copy(grad_hbm.at[pl.ds(first, chunk)], gbuf.at[i], g_sem.at[i]),
            pltpu.make_async_copy(act_hbm.at[pl.ds(first, chunk)], abuf.at[i], a_sem.at[i]),
        ))
        loads[-1][0].start()
        loads[-1][1].start()

    wout[pl.ds(PROJ, PROJ)] = jnp.zeros((PROJ, wout.shape[1]), BF16)
    win[pl.ds(0, PROJ)] = jnp.zeros((PROJ, win.shape[1]), BF16)
    xacc[...] = jnp.zeros_like(xacc)
    for copy in weights:
        copy.wait()
    wt_out[...] = wout[...].T
    wt_in[...] = win[...].T

    def project(group):
        for i in group:
            loads[i][0].wait()
            loads[i][1].wait()
        total = {}
        for source, weight in ((gbuf, wt_out), (abuf, wt_in)):
            for first in range(0, weight.shape[0], DEPTH):
                for i in group:
                    term = jnp.dot(
                        source[i, :, pl.ds(first, DEPTH)], weight[pl.ds(first, DEPTH)],
                        preferred_element_type=F32,
                    )
                    total[i] = total[i] + term if i in total else term
        for i in group:
            part[i] = total[i].reshape((2, 2, nt // 2, LANES))

    ahead = 3
    project(range(ahead))
    pl.semaphore_wait(barrier, len(greeted))
    for device in line:
        pl.semaphore_signal(ready, inc=1, device_id=device, device_id_type=MESH)

    sib = [
        remote(part.at[i, 1 - c], sib_recv.at[i], sib_s.at[i], sib_r.at[i], sibling)
        for i in range(nz)
    ]
    at = {order(i) - nz if order(i) > 4 else order(i): i for i in range(nz)}
    sides = (1, -1)

    def far(s, h):
        n = 2 * s + h
        return remote(
            sums.at[at[3 * sides[s]], h], far_recv.at[s, h], far_s.at[n], far_r.at[n], zdev(sides[s])
        )

    def farthest(s):
        return remote(
            sums.at[at[4], s], far_recv.at[2, s], far_s.at[4 + s], far_r.at[4 + s], zdev(2 * sides[s])
        )

    def near(s):
        return remote(sums.at[at[sides[s]]], near_recv.at[s], near_s.at[s], near_r.at[s], zdev(sides[s]))

    def second(s, h):
        n = 2 + 2 * s + h
        return remote(
            sums.at[at[2 * sides[s]], h], near_recv.at[2 + s, h], near_s.at[n], near_r.at[n],
            zdev(2 * sides[s]),
        )

    for i in range(ahead):
        sib[i].start()
    groups = {3: (3, 4), 5: (5, 6, 7)}
    for i in range(nz):
        if i in groups:
            project(groups[i])
            for later in groups[i]:
                sib[later].start()
        sib[i].wait_recv()
        sums[i] = part[i, c] + sib_recv[i]
        if i == at[4]:
            farthest(0).start()
            farthest(1).start()
        for s in range(2):
            if i == at[3 * sides[s]]:
                far(s, 1 - s).start()
                far(s, s).start()
            if i == at[sides[s]]:
                near(s).start()
    for s in range(2):
        far(s, 1 - s).wait_recv()
        sums[at[2 * sides[s]], 1 - s] += far_recv[s, 1 - s]
        second(s, 1 - s).start()
    for s in range(2):
        far(s, s).wait_recv()
        farthest(s).wait_recv()
        sums[at[2 * sides[s]], s] += far_recv[s, s] + far_recv[2, s]
        second(s, s).start()
    for s in range(2):
        near(s).wait_recv()
    tok[z, c] = sums[at[0]] + (near_recv[0] + near_recv[1])
    for h in range(2):
        second(0, h).wait_recv()
        second(1, h).wait_recv()
        tok[z, c, h] += near_recv[2, h] + near_recv[3, h]

    def owner(k):
        return ring[k % nz]

    def spread(s, h):
        n = 2 * s + h
        return remote(tok.at[z, c, h], tok.at[z, c, h], ag_s.at[n], ag_r.at[n], zdev(2 * sides[s]))

    def beside(s):
        return remote(tok.at[z, c], tok.at[z, c], ag_s.at[4 + s], ag_r.at[4 + s], zdev(sides[s]))

    def onward(s, h):
        n = 2 * s + h
        mine = tok.at[owner(-2 * sides[s]), c, h]
        return remote(mine, mine, fa_s.at[n], fa_r.at[n], zdev(sides[s]))

    def opposite(s):
        mine = tok.at[owner(-2 * sides[s]), c, s]
        return remote(mine, mine, fa_s.at[4 + s], fa_r.at[4 + s], zdev(2 * sides[s]))

    for first in range(2):
        for s in range(2):
            spread(s, s if first == 0 else 1 - s).start()
    for s in range(2):
        beside(s).start()

    lane = lax.broadcasted_iota(jnp.int32, (nt, LANES), 1)
    example = lax.broadcasted_iota(jnp.int32, (EXAMPLES, nt), 0)

    def share(k):
        mine = tok.at[owner(k), c]
        return remote(mine, mine, sh_s.at[k % nz], sh_r.at[k % nz], sibling)

    def accumulate(k, core):
        chip = owner(k)
        whole = tok[chip, core].reshape(nt, LANES)
        flipped = whole.T
        high = flipped[:PROJ].astype(BF16).astype(F32)
        high_ref[...] = high
        low_ref[...] = flipped[:PROJ] - high
        first = pl.multiple_of(chip * chunk + core * nt, nt)
        member = seg[:, pl.ds(first, nt)] == example
        even = jnp.where(lane < PROJ, pltpu.roll(whole, PROJ, 1), 0.0)
        odd = jnp.where(lane < PROJ, 0.0, whole)
        in_high, in_low = split(jnp.concatenate([even, odd], axis=0))
        both = jnp.concatenate([in_high, in_low], axis=1)

        def weigh(ref, p):
            pair = [
                jnp.where(member, jnp.broadcast_to(ref[pl.ds(p + parity, 1), :], member.shape), 0.0)
                for parity in range(2)
            ]
            return jnp.concatenate(pair, axis=1).astype(BF16)

        for part_of in range(2):
            ps = [8 * zz + 4 * c + 2 * jj for zz in range(4 * part_of, 4 * part_of + 4) for jj in range(2)]
            w_high = jnp.concatenate([weigh(high_ref, p) for p in ps], axis=0)
            w_low = jnp.concatenate([weigh(low_ref, p) for p in ps], axis=0)
            one = jnp.dot(w_high, both, preferred_element_type=F32)
            two = jnp.dot(w_low, in_high, preferred_element_type=F32)
            block = one[:, :LANES] + (one[:, LANES:] + two)
            xacc[pl.ds(4 * part_of, 4)] += block.reshape(4, 2 * EXAMPLES, LANES)

    def own(k):
        accumulate(k, c)

    def others(k):
        share(k).wait_recv()
        accumulate(k, 1 - c)

    share(0).start()
    own(0)
    others(0)
    for s in range(2):
        spread(s, s).wait_recv()
        opposite(s).start()
        onward(s, s).start()
    for s in range(2):
        spread(s, 1 - s).wait_recv()
        onward(s, 1 - s).start()
        share(-2 * sides[s]).start()
    for s in range(2):
        own(-2 * sides[s])
    for s in range(2):
        beside(s).wait_recv()
        share(-sides[s]).start()
    for s in range(2):
        own(-sides[s])
    for s in range(2):
        others(-2 * sides[s])
    for s in range(2):
        others(-sides[s])
    for s in range(2):
        for h in range(2):
            onward(s, h).wait_recv()
        share(-3 * sides[s]).start()
    for s in range(2):
        opposite(s).wait_recv()
    share(4).start()
    for s in range(2):
        own(-3 * sides[s])
    own(4)
    for s in range(2):
        others(-3 * sides[s])
    others(4)

    squares = xacc[...] * xacc[...]
    ss[...] = jnp.sum(squares.reshape(-1, LANES), axis=0, keepdims=True)
    pl.semaphore_wait(ready, len(line))

    home = lax.div(d, 2)
    forwards = c == lax.rem(d, 2)
    places = [lax.rem(home + m, ndp // 2) for m in range(ndp // 2)]

    def column(m):
        place = places[m]
        return remote(
            xacc.at[place], cols.at[d], col_s.at[m], col_r.at[d], (2 * place + c, t)
        )

    def column_from(source):
        return remote(xacc.at[0], cols.at[source], col_s.at[0], col_r.at[source], (source, t))

    def forward(source):
        return remote(cols.at[source], cols.at[source], fw_s.at[source], fw_r.at[source], sibling)

    def row(k):
        return remote(xacc.at[z], rows.at[d], row_s.at[k], row_r.at[d], (plane[k], t))

    def row_from(source):
        return remote(xacc.at[z], rows.at[source], row_s.at[1], row_r.at[source], (source, t))

    def square(k):
        return remote(ss, ss_all.at[d], sq_s.at[k], sq_r.at[d], (plane[k], t))

    def square_from(source):
        return remote(ss, ss_all.at[source], sq_s.at[1], sq_r.at[source], (source, t))

    for m in range(1, ndp // 2):
        column(m).start()

    @pl.when(jnp.logical_not(forwards))
    def _():
        column(0).start()

    for k in range(1, ndp):
        square(k).start()
    for k in range(1, ndp):
        row(k).start()
    rows[d] = xacc[z]
    ss_all[d] = ss[...]

    @pl.when(forwards)
    def _():
        cols[d] = xacc[home]
        forward(d).start()
        for k in range(1, ndp):
            source = plane[k]
            column_from(source).wait_recv()
            forward(source).start()

    for k in range(1, ndp):
        square_from(plane[k]).wait_recv()
    ss_sum[...] = jnp.sum(ss_all[...], axis=0)
    swap_ss = remote(ss_sum, ss_recv, ss_sem.at[0], ss_sem.at[1], sibling)
    swap_ss.start()
    for k in range(1, ndp):
        row_from(plane[k]).wait_recv()

    def matrix(ref, out):
        for jj in range(2):
            out[:, pl.ds(jj * LANES, LANES)] = ref[:, pl.ds(jj * EXAMPLES, EXAMPLES), :].reshape(
                ndp * EXAMPLES, LANES
            )

    matrix(rows, left_ref)

    @pl.when(jnp.logical_not(forwards))
    def _():
        for k in range(ndp):
            forward(plane[k]).wait_recv()

    matrix(cols, right_ref)
    swap_ss.wait_recv()
    trace = jnp.sum(ss_sum[...] + ss_recv[...], keepdims=True)
    scale_ref[...] = trace / (PROJ * PROJ) + 1e-6

    for copy in sib + [swap_ss] + [share(k) for k in range(nz)]:
        copy.wait_send()
    for s in range(2):
        for copy in (farthest(s), near(s), beside(s), opposite(s)):
            copy.wait_send()
        for h in range(2):
            for copy in (far(s, h), second(s, h), spread(s, h), onward(s, h)):
                copy.wait_send()
    for m in range(1, ndp // 2):
        column(m).wait_send()
    for k in range(1, ndp):
        row(k).wait_send()
        square(k).wait_send()

    @pl.when(forwards)
    def _():
        for k in range(ndp):
            forward(k).wait_send()

    @pl.when(jnp.logical_not(forwards))
    def _():
        column(0).wait_send()


def shards(ndp, nz, grad_up, activations, segment_ids, proj_out, proj_in):
    tokens, hidden = grad_up.shape
    features = activations.shape[1]
    nt = tokens // (2 * nz)
    rows = 2 * EXAMPLES
    block = 4 * PROJ
    dma = pltpu.SemaphoreType.DMA
    halves = (2, nt // 2, LANES)
    arrays = (grad_up, activations, segment_ids, proj_out, proj_in)
    in_hbm = [pltpu.with_memory_space_constraint(array, pltpu.HBM) for array in arrays]
    left, right, scale = pl.pallas_call(
        functools.partial(kernel, ndp, nz, nt),
        out_shape=[
            jax.ShapeDtypeStruct((ndp * EXAMPLES, block), F32),
            jax.ShapeDtypeStruct((ndp * EXAMPLES, block), F32),
            jax.ShapeDtypeStruct((1, 1), F32),
        ],
        in_specs=[pl.BlockSpec(memory_space=pltpu.HBM)] * 5,
        out_specs=[pl.BlockSpec(memory_space=pltpu.VMEM)] * 3,
        scratch_shapes=[
            pltpu.VMEM((nz, 2 * nt, hidden), BF16),
            pltpu.VMEM((nz, 2 * nt, features), BF16),
            pltpu.VMEM((1, tokens), jnp.int32),
            pltpu.VMEM((2 * PROJ, hidden), BF16),
            pltpu.VMEM((2 * PROJ, features), BF16),
            pltpu.VMEM((hidden, 2 * PROJ), BF16),
            pltpu.VMEM((features, 2 * PROJ), BF16),
            pltpu.VMEM((nz, 2) + halves, F32),
            pltpu.VMEM((nz,) + halves, F32),
            pltpu.VMEM((nz,) + halves, F32),
            pltpu.VMEM((3,) + halves, F32),
            pltpu.VMEM((4,) + halves, F32),
            pltpu.VMEM((nz, 2) + halves, F32),
            pltpu.VMEM((PROJ, nt), F32),
            pltpu.VMEM((PROJ, nt), F32),
            pltpu.VMEM((nz, rows, LANES), F32),
            pltpu.VMEM((ndp, rows, LANES), F32),
            pltpu.VMEM((ndp, rows, LANES), F32),
            pltpu.VMEM((1, LANES), F32),
            pltpu.VMEM((ndp, 1, LANES), F32),
            pltpu.VMEM((1, LANES), F32),
            pltpu.VMEM((1, LANES), F32),
            dma((nz,)), dma((nz,)), dma((3,)),
            dma((nz,)), dma((nz,)), dma((6,)), dma((6,)), dma((6,)), dma((6,)),
            dma((6,)), dma((6,)), dma((6,)), dma((6,)), dma((nz,)), dma((nz,)),
            dma((ndp,)), dma((ndp,)), dma((ndp,)), dma((ndp,)), dma((ndp,)), dma((ndp,)),
            dma((ndp,)), dma((ndp,)), dma((2,)), pltpu.SemaphoreType.REGULAR,
        ],
        compiler_params=pltpu.CompilerParams(
            collective_id=0, has_side_effects=True, vmem_limit_bytes=24 * 2**20
        ),
        cost_estimate=pl.CostEstimate(
            flops=2 * tokens * (hidden + features) * PROJ,
            bytes_accessed=2 * tokens * (hidden + features),
            transcendentals=0,
        ),
    )(*in_hbm)
    raw = lax.dot_general(
        left, right, (((0,), (0,)), ((), ())),
        precision=lax.Precision.HIGHEST, preferred_element_type=F32,
    )
    return raw / scale[0, 0]


def solution(mesh):
    in_specs = (
        P("dp", "tensor"),
        P("dp", "tensor"),
        P("dp", None),
        P(None, "tensor"),
        P(None, "tensor"),
    )
    body = functools.partial(shards, mesh.shape["dp"], mesh.shape["tensor"] // 2)
    return jax.shard_map(
        body, mesh=mesh, in_specs=in_specs, out_specs=P("tensor", "dp"), check_vma=False
    )
```

```python
import functools

import jax
import jax.numpy as jnp
from jax import lax
from jax.experimental import pallas as pl
from jax.experimental.pallas import tpu as pltpu
from jax.sharding import PartitionSpec as P

MESH = pl.DeviceIdType.MESH
F32 = jnp.float32
BF16 = jnp.bfloat16
EXAMPLES = 16
PROJ = 64
LANES = 128
DEPTH = 256
SIDE = 4


def split(x):
    high = x.astype(BF16)
    low = (x - high.astype(F32)).astype(BF16)
    return high, low


ORDER = (4, 3, -3, 1, -1, 2, -2, 0)
GROUPS = ((0, 1, 2), (3, 4), (5, 6), (7,))


def kernel(
    ndp, nz, nt,
    grad_hbm, act_hbm, seg_hbm, po_hbm, pi_hbm, left_ref, right_ref, scale_ref,
    gbuf, abuf, seg, wout, win, wt_out, wt_in, part, sib_recv, sums, far_recv, last_recv, near_recv, tok,
    high_ref, low_ref, xacc, message, rows, cols, ss_sum, ss_recv,
    g_sem, a_sem, w_sem, sib_s, sib_r, far_s, far_r, near_s, near_r, ag_s, ag_r, fa_s, fa_r,
    sh_s, sh_r, row_s, row_r, col_s, col_r, fw_s, fw_r, ss_sem, ready,
):
    d = lax.axis_index("dp")
    t = lax.axis_index("tensor")
    z, c = lax.div(t, 2), lax.rem(t, 2)
    ring = [lax.rem(z + k, nz) for k in range(nz)]
    plane = [lax.rem(d + k, ndp) for k in range(ndp)]
    sibling = (d, t + 1 - 2 * c)
    chunk = 2 * nt

    def zdev(k):
        return (d, ring[k % nz] * 2 + c)

    def remote(src, dst, send, recv, device):
        return pltpu.make_async_remote_copy(
            src_ref=src, dst_ref=dst, send_sem=send, recv_sem=recv,
            device_id=device, device_id_type=MESH,
        )

    barrier = pltpu.get_barrier_semaphore()
    line = [(lax.div(d, SIDE) * SIDE + lax.rem(d + k, SIDE), t) for k in range(1, SIDE)]
    column_peers = [(plane[SIDE * k], t) for k in range(1, ndp // SIDE)]
    greeted = [zdev(k) for k in (1, -1, 2, -2)] + line + column_peers + [sibling]
    for device in greeted:
        pl.semaphore_signal(barrier, inc=1, device_id=device, device_id_type=MESH)

    weights = [
        pltpu.make_async_copy(po_hbm, wout.at[pl.ds(0, PROJ)], w_sem.at[0]),
        pltpu.make_async_copy(pi_hbm, win.at[pl.ds(PROJ, PROJ)], w_sem.at[1]),
        pltpu.make_async_copy(seg_hbm, seg, w_sem.at[2]),
    ]
    for copy in weights:
        copy.start()
    loads = []
    for i in range(nz):
        first = pl.multiple_of(ring[ORDER[i] % nz] * chunk, chunk)
        loads.append((
            pltpu.make_async_copy(grad_hbm.at[pl.ds(first, chunk)], gbuf.at[i], g_sem.at[i]),
            pltpu.make_async_copy(act_hbm.at[pl.ds(first, chunk)], abuf.at[i], a_sem.at[i]),
        ))
    for i in GROUPS[0]:
        loads[i][0].start()
        loads[i][1].start()

    wout[pl.ds(PROJ, PROJ)] = jnp.zeros((PROJ, wout.shape[1]), BF16)
    win[pl.ds(0, PROJ)] = jnp.zeros((PROJ, win.shape[1]), BF16)
    xacc[...] = jnp.zeros_like(xacc)
    for copy in weights:
        copy.wait()
    wt_out[...] = wout[...].T
    wt_in[...] = win[...].T

    def project(group):
        for i in group:
            loads[i][0].wait()
            loads[i][1].wait()
        if group == GROUPS[0]:
            for i in range(len(group), nz):
                loads[i][0].start()
                loads[i][1].start()
        total = {}
        for source, weight in ((gbuf, wt_out), (abuf, wt_in)):
            for first in range(0, weight.shape[0], DEPTH):
                for i in group:
                    term = jnp.dot(
                        source[i, :, pl.ds(first, DEPTH)], weight[pl.ds(first, DEPTH)],
                        preferred_element_type=F32,
                    )
                    total[i] = total[i] + term if i in total else term
        for i in group:
            part[i] = total[i].reshape((2, 2, nt // 2, LANES))

    project(GROUPS[0])
    pl.semaphore_wait(barrier, len(greeted))
    for device in line:
        pl.semaphore_signal(ready, inc=1, device_id=device, device_id_type=MESH)

    sib = [
        remote(part.at[i, 1 - c], sib_recv.at[i], sib_s.at[i], sib_r.at[i], sibling)
        for i in range(nz)
    ]
    at = {offset: i for i, offset in enumerate(ORDER)}
    sides = (1, -1)
    quarter = nt // 4

    def far(s, h):
        n = 2 * s + h
        return remote(
            sums.at[at[3 * sides[s]], h], far_recv.at[s, h], far_s.at[n], far_r.at[n], zdev(sides[s])
        )

    def farthest(s, h):
        n = 4 + 2 * s + h
        return remote(
            sums.at[at[4], h, pl.ds(s * quarter, quarter)], last_recv.at[s, h], far_s.at[n], far_r.at[n],
            zdev(2 * sides[s]),
        )

    def near(s):
        return remote(sums.at[at[sides[s]]], near_recv.at[s], near_s.at[s], near_r.at[s], zdev(sides[s]))

    def second(s, h):
        n = 2 + 2 * s + h
        return remote(
            sums.at[at[2 * sides[s]], h], near_recv.at[2 + s, h], near_s.at[n], near_r.at[n],
            zdev(2 * sides[s]),
        )

    for i in GROUPS[0]:
        sib[i].start()
    for n, group in enumerate(GROUPS):
        if 0 < n < len(GROUPS) - 1:
            project(GROUPS[n + 1])
            for i in GROUPS[n + 1]:
                sib[i].start()
        for i in group:
            sib[i].wait_recv()
            sums[i] = part[i, c] + sib_recv[i]
            for s in range(2):
                if i == at[sides[s]]:
                    near(s).start()
        if n == 0:
            for h in range(2):
                for s in range(2):
                    farthest(s, h).start()
                for s in range(2):
                    far(s, h).start()
            project(GROUPS[1])
            for i in GROUPS[1]:
                sib[i].start()
    def owner(k):
        return ring[k % nz]

    def spread(s, h):
        n = 2 * s + h
        return remote(tok.at[z, c, h], tok.at[z, c, h], ag_s.at[n], ag_r.at[n], zdev(2 * sides[s]))

    def beside(s):
        return remote(tok.at[z, c], tok.at[z, c], ag_s.at[4 + s], ag_r.at[4 + s], zdev(sides[s]))

    def onward(s, h):
        n = 2 * s + h
        mine = tok.at[owner(-2 * sides[s]), c, h]
        return remote(mine, mine, fa_s.at[n], fa_r.at[n], zdev(sides[s]))

    def opposite(s, h):
        n = 4 + 2 * s + h
        mine = tok.at[owner(-2 * sides[s]), c, h, pl.ds(s * quarter, quarter)]
        return remote(mine, mine, fa_s.at[n], fa_r.at[n], zdev(2 * sides[s]))

    for h in range(2):
        for s in range(2):
            mine = pl.ds(s * quarter, quarter)
            far(s, h).wait_recv()
            sums[at[2 * sides[s]], h] += far_recv[s, h]
            farthest(s, h).wait_recv()
            sums[at[2 * sides[s]], h, mine] += last_recv[s, h]
            second(s, h).start()
    for s in range(2):
        near(s).wait_recv()
    for h in range(2):
        beside_sums = sums[at[0], h] + (near_recv[0, h] + near_recv[1, h])
        for s in range(2):
            second(s, h).wait_recv()
        tok[z, c, h] = beside_sums + (near_recv[2, h] + near_recv[3, h])
        for s in range(2):
            spread(s, h).start()
    for s in range(2):
        beside(s).start()

    lane = lax.broadcasted_iota(jnp.int32, (nt, LANES), 1)
    example = lax.broadcasted_iota(jnp.int32, (EXAMPLES, nt), 0)

    def share(k):
        mine = tok.at[owner(k), c]
        return remote(mine, mine, sh_s.at[k % nz], sh_r.at[k % nz], sibling)

    def accumulate(k, core):
        chip = owner(k)
        whole = tok[chip, core].reshape(nt, LANES)
        flipped = whole.T
        high = flipped[:PROJ].astype(BF16).astype(F32)
        high_ref[...] = high
        low_ref[...] = flipped[:PROJ] - high
        first = pl.multiple_of(chip * chunk + core * nt, nt)
        member = seg[:, pl.ds(first, nt)] == example
        even = jnp.where(lane < PROJ, pltpu.roll(whole, PROJ, 1), 0.0)
        odd = jnp.where(lane < PROJ, 0.0, whole)
        in_high, in_low = split(jnp.concatenate([even, odd], axis=0))
        both = jnp.concatenate([in_high, in_low], axis=1)

        def weigh(ref, p):
            pair = [
                jnp.where(member, jnp.broadcast_to(ref[pl.ds(p + parity, 1), :], member.shape), 0.0)
                for parity in range(2)
            ]
            return jnp.concatenate(pair, axis=1).astype(BF16)

        for part_of in range(2):
            ps = [8 * zz + 4 * c + 2 * jj for zz in range(4 * part_of, 4 * part_of + 4) for jj in range(2)]
            w_high = jnp.concatenate([weigh(high_ref, p) for p in ps], axis=0)
            w_low = jnp.concatenate([weigh(low_ref, p) for p in ps], axis=0)
            one = jnp.dot(w_high, both, preferred_element_type=F32)
            two = jnp.dot(w_low, in_high, preferred_element_type=F32)
            block = one[:, :LANES] + (one[:, LANES:] + two)
            xacc[pl.ds(4 * part_of, 4)] += block.reshape(4, 2 * EXAMPLES, LANES)

    def own(k):
        accumulate(k, c)

    def others(k):
        share(k).wait_recv()
        accumulate(k, 1 - c)

    share(0).start()
    own(0)
    others(0)
    for h in range(2):
        for s in range(2):
            spread(s, h).wait_recv()
            opposite(s, h).start()
            onward(s, h).start()
    for s in range(2):
        share(-2 * sides[s]).start()
    for s in range(2):
        own(-2 * sides[s])
    for s in range(2):
        beside(s).wait_recv()
        share(-sides[s]).start()
    for s in range(2):
        own(-sides[s])
    for s in range(2):
        others(-2 * sides[s])
    for s in range(2):
        others(-sides[s])
    for s in range(2):
        for h in range(2):
            onward(s, h).wait_recv()
        share(-3 * sides[s]).start()
    own(-3 * sides[0])
    for s in range(2):
        for h in range(2):
            opposite(s, h).wait_recv()
    share(4).start()
    own(-3 * sides[1])
    own(4)
    for s in range(2):
        others(-3 * sides[s])
    others(4)

    squares = xacc[...] * xacc[...]
    message[pl.ds(0, 2 * EXAMPLES)] = xacc[z]
    message[pl.ds(2 * EXAMPLES, 1)] = jnp.sum(squares.reshape(-1, LANES), axis=0, keepdims=True)
    pl.semaphore_wait(ready, len(line))

    home = lax.div(d, 2)
    forwards = c == lax.rem(d, 2)
    places = [lax.rem(home + m, ndp // 2) for m in range(ndp // 2)]

    def column(m):
        place = places[m]
        return remote(
            xacc.at[place], cols.at[d], col_s.at[m], col_r.at[d], (2 * place + c, t)
        )

    def column_from(source):
        return remote(xacc.at[0], cols.at[source], col_s.at[0], col_r.at[source], (source, t))

    def forward(source):
        return remote(cols.at[source], cols.at[source], fw_s.at[source], fw_r.at[source], sibling)

    sent = message.at[pl.ds(0, 2 * EXAMPLES + 1)]

    def row(k):
        return remote(
            sent, rows.at[d, pl.ds(0, 2 * EXAMPLES + 1)], row_s.at[k], row_r.at[d], (plane[k], t)
        )

    def row_from(source):
        return remote(
            sent, rows.at[source, pl.ds(0, 2 * EXAMPLES + 1)], row_s.at[1], row_r.at[source], (source, t)
        )

    for m in range(1, ndp // 2):
        column(m).start()

    @pl.when(jnp.logical_not(forwards))
    def _():
        column(0).start()

    for k in range(1, ndp):
        row(k).start()
    rows[d, pl.ds(0, 2 * EXAMPLES + 1)] = message[pl.ds(0, 2 * EXAMPLES + 1)]

    @pl.when(forwards)
    def _():
        cols[d] = xacc[home]
        forward(d).start()
        for k in range(1, ndp):
            source = plane[k]
            column_from(source).wait_recv()
            forward(source).start()

    for k in range(1, ndp):
        row_from(plane[k]).wait_recv()
    ss_sum[...] = jnp.sum(rows[:, pl.ds(2 * EXAMPLES, 1), :], axis=0)
    swap_ss = remote(ss_sum, ss_recv, ss_sem.at[0], ss_sem.at[1], sibling)
    swap_ss.start()

    def matrix(ref, out):
        for jj in range(2):
            out[:, pl.ds(jj * LANES, LANES)] = ref[:, pl.ds(jj * EXAMPLES, EXAMPLES), :].reshape(
                ndp * EXAMPLES, LANES
            )

    matrix(rows, left_ref)

    @pl.when(jnp.logical_not(forwards))
    def _():
        for k in range(ndp):
            forward(plane[k]).wait_recv()

    matrix(cols, right_ref)
    swap_ss.wait_recv()
    trace = jnp.sum(ss_sum[...] + ss_recv[...], keepdims=True)
    scale_ref[...] = trace / (PROJ * PROJ) + 1e-6

    for copy in sib + [swap_ss] + [share(k) for k in range(nz)]:
        copy.wait_send()
    for s in range(2):
        for copy in (near(s), beside(s)):
            copy.wait_send()
        for h in range(2):
            for copy in (
                far(s, h), farthest(s, h), second(s, h), spread(s, h), onward(s, h), opposite(s, h)
            ):
                copy.wait_send()
    for m in range(1, ndp // 2):
        column(m).wait_send()
    for k in range(1, ndp):
        row(k).wait_send()

    @pl.when(forwards)
    def _():
        for k in range(ndp):
            forward(k).wait_send()

    @pl.when(jnp.logical_not(forwards))
    def _():
        column(0).wait_send()


def shards(ndp, nz, grad_up, activations, segment_ids, proj_out, proj_in):
    tokens, hidden = grad_up.shape
    features = activations.shape[1]
    nt = tokens // (2 * nz)
    rows = 2 * EXAMPLES
    block = 4 * PROJ
    dma = pltpu.SemaphoreType.DMA
    halves = (2, nt // 2, LANES)
    arrays = (grad_up, activations, segment_ids, proj_out, proj_in)
    in_hbm = [pltpu.with_memory_space_constraint(array, pltpu.HBM) for array in arrays]
    left, right, scale = pl.pallas_call(
        functools.partial(kernel, ndp, nz, nt),
        out_shape=[
            jax.ShapeDtypeStruct((ndp * EXAMPLES, block), F32),
            jax.ShapeDtypeStruct((ndp * EXAMPLES, block), F32),
            jax.ShapeDtypeStruct((1, 1), F32),
        ],
        in_specs=[pl.BlockSpec(memory_space=pltpu.HBM)] * 5,
        out_specs=[pl.BlockSpec(memory_space=pltpu.VMEM)] * 3,
        scratch_shapes=[
            pltpu.VMEM((nz, 2 * nt, hidden), BF16),
            pltpu.VMEM((nz, 2 * nt, features), BF16),
            pltpu.VMEM((1, tokens), jnp.int32),
            pltpu.VMEM((2 * PROJ, hidden), BF16),
            pltpu.VMEM((2 * PROJ, features), BF16),
            pltpu.VMEM((hidden, 2 * PROJ), BF16),
            pltpu.VMEM((features, 2 * PROJ), BF16),
            pltpu.VMEM((nz, 2) + halves, F32),
            pltpu.VMEM((nz,) + halves, F32),
            pltpu.VMEM((nz,) + halves, F32),
            pltpu.VMEM((2,) + halves, F32),
            pltpu.VMEM((2, 2, nt // 4, LANES), F32),
            pltpu.VMEM((4,) + halves, F32),
            pltpu.VMEM((nz, 2) + halves, F32),
            pltpu.VMEM((PROJ, nt), F32),
            pltpu.VMEM((PROJ, nt), F32),
            pltpu.VMEM((nz, rows, LANES), F32),
            pltpu.VMEM((rows + 8, LANES), F32),
            pltpu.VMEM((ndp, rows + 8, LANES), F32),
            pltpu.VMEM((ndp, rows, LANES), F32),
            pltpu.VMEM((1, LANES), F32),
            pltpu.VMEM((1, LANES), F32),
            dma((nz,)), dma((nz,)), dma((3,)),
            dma((nz,)), dma((nz,)), dma((8,)), dma((8,)), dma((6,)), dma((6,)),
            dma((6,)), dma((6,)), dma((8,)), dma((8,)), dma((nz,)), dma((nz,)),
            dma((ndp,)), dma((ndp,)), dma((ndp,)), dma((ndp,)), dma((ndp,)), dma((ndp,)),
            dma((2,)), pltpu.SemaphoreType.REGULAR,
        ],
        compiler_params=pltpu.CompilerParams(
            collective_id=0, has_side_effects=True, vmem_limit_bytes=24 * 2**20
        ),
        cost_estimate=pl.CostEstimate(
            flops=2 * tokens * (hidden + features) * PROJ,
            bytes_accessed=2 * tokens * (hidden + features),
            transcendentals=0,
        ),
    )(*in_hbm)
    raw = lax.dot_general(
        left, right, (((0,), (0,)), ((), ())),
        precision=lax.Precision.HIGHEST, preferred_element_type=F32,
    )
    return raw / scale[0, 0]


def solution(mesh):
    in_specs = (
        P("dp", "tensor"),
        P("dp", "tensor"),
        P("dp", None),
        P(None, "tensor"),
        P(None, "tensor"),
    )
    body = functools.partial(shards, mesh.shape["dp"], mesh.shape["tensor"] // 2)
    return jax.shard_map(
        body, mesh=mesh, in_specs=in_specs, out_specs=P("tensor", "dp"), check_vma=False
    )
```

```python
import functools

import jax
import jax.numpy as jnp
from jax import lax
from jax.experimental import pallas as pl
from jax.experimental.pallas import tpu as pltpu
from jax.sharding import PartitionSpec as P

MESH = pl.DeviceIdType.MESH
F32 = jnp.float32
BF16 = jnp.bfloat16
EXAMPLES = 16
PROJ = 64
LANES = 128
DEPTH = 256
SIDE = 4


def split(x):
    high = x.astype(BF16)
    low = (x - high.astype(F32)).astype(BF16)
    return high, low


ORDER = (4, 3, -3, 1, -1, 2, -2, 0)
GROUPS = ((0, 1, 2), (3, 4), (5, 6), (7,))


def kernel(
    ndp, nz, nt,
    grad_hbm, act_hbm, seg_hbm, po_hbm, pi_hbm, left_ref, right_ref,
    gbuf, abuf, seg, wout, win, wt_out, wt_in, part, sib_recv, sums, far_recv, last_recv, near_recv, tok,
    high_ref, low_ref, xacc, message, rows, cols, ss_sum, ss_recv,
    g_sem, a_sem, w_sem, sib_s, sib_r, far_s, far_r, near_s, near_r, ag_s, ag_r, fa_s, fa_r,
    sh_s, sh_r, row_s, row_r, col_s, col_r, fw_s, fw_r, ss_sem, ready,
):
    d = lax.axis_index("dp")
    t = lax.axis_index("tensor")
    z, c = lax.div(t, 2), lax.rem(t, 2)
    ring = [lax.rem(z + k, nz) for k in range(nz)]
    plane = [lax.rem(d + k, ndp) for k in range(ndp)]
    sibling = (d, t + 1 - 2 * c)
    chunk = 2 * nt

    def zdev(k):
        return (d, ring[k % nz] * 2 + c)

    def remote(src, dst, send, recv, device):
        return pltpu.make_async_remote_copy(
            src_ref=src, dst_ref=dst, send_sem=send, recv_sem=recv,
            device_id=device, device_id_type=MESH,
        )

    barrier = pltpu.get_barrier_semaphore()
    line = [(lax.div(d, SIDE) * SIDE + lax.rem(d + k, SIDE), t) for k in range(1, SIDE)]
    column_peers = [(plane[SIDE * k], t) for k in range(1, ndp // SIDE)]
    greeted = [zdev(k) for k in (1, -1, 2, -2)] + line + column_peers + [sibling]
    for device in greeted:
        pl.semaphore_signal(barrier, inc=1, device_id=device, device_id_type=MESH)

    weights = [
        pltpu.make_async_copy(po_hbm, wout.at[pl.ds(0, PROJ)], w_sem.at[0]),
        pltpu.make_async_copy(pi_hbm, win.at[pl.ds(PROJ, PROJ)], w_sem.at[1]),
        pltpu.make_async_copy(seg_hbm, seg, w_sem.at[2]),
    ]
    for copy in weights:
        copy.start()
    loads = []
    for i in range(nz):
        first = pl.multiple_of(ring[ORDER[i] % nz] * chunk, chunk)
        loads.append((
            pltpu.make_async_copy(grad_hbm.at[pl.ds(first, chunk)], gbuf.at[i], g_sem.at[i]),
            pltpu.make_async_copy(act_hbm.at[pl.ds(first, chunk)], abuf.at[i], a_sem.at[i]),
        ))
    for i in GROUPS[0]:
        loads[i][0].start()
        loads[i][1].start()

    wout[pl.ds(PROJ, PROJ)] = jnp.zeros((PROJ, wout.shape[1]), BF16)
    win[pl.ds(0, PROJ)] = jnp.zeros((PROJ, win.shape[1]), BF16)
    xacc[...] = jnp.zeros_like(xacc)
    for copy in weights:
        copy.wait()
    wt_out[...] = wout[...].T
    wt_in[...] = win[...].T

    def project(group):
        for i in group:
            loads[i][0].wait()
            loads[i][1].wait()
        if group == GROUPS[0]:
            for i in range(len(group), nz):
                loads[i][0].start()
                loads[i][1].start()
        total = {}
        for source, weight in ((gbuf, wt_out), (abuf, wt_in)):
            for first in range(0, weight.shape[0], DEPTH):
                for i in group:
                    term = jnp.dot(
                        source[i, :, pl.ds(first, DEPTH)], weight[pl.ds(first, DEPTH)],
                        preferred_element_type=F32,
                    )
                    total[i] = total[i] + term if i in total else term
        for i in group:
            part[i] = total[i].reshape((2, 2, nt // 2, LANES))

    project(GROUPS[0])
    pl.semaphore_wait(barrier, len(greeted))
    for device in line:
        pl.semaphore_signal(ready, inc=1, device_id=device, device_id_type=MESH)

    sib = [
        remote(part.at[i, 1 - c], sib_recv.at[i], sib_s.at[i], sib_r.at[i], sibling)
        for i in range(nz)
    ]
    at = {offset: i for i, offset in enumerate(ORDER)}
    sides = (1, -1)
    quarter = nt // 4

    def far(s, h):
        n = 2 * s + h
        return remote(
            sums.at[at[3 * sides[s]], h], far_recv.at[s, h], far_s.at[n], far_r.at[n], zdev(sides[s])
        )

    def farthest(s, h):
        n = 4 + 2 * s + h
        return remote(
            sums.at[at[4], h, pl.ds(s * quarter, quarter)], last_recv.at[s, h], far_s.at[n], far_r.at[n],
            zdev(2 * sides[s]),
        )

    def near(s):
        return remote(sums.at[at[sides[s]]], near_recv.at[s], near_s.at[s], near_r.at[s], zdev(sides[s]))

    def second(s, h):
        n = 2 + 2 * s + h
        return remote(
            sums.at[at[2 * sides[s]], h], near_recv.at[2 + s, h], near_s.at[n], near_r.at[n],
            zdev(2 * sides[s]),
        )

    for i in GROUPS[0]:
        sib[i].start()
    for n, group in enumerate(GROUPS):
        if 0 < n < len(GROUPS) - 1:
            project(GROUPS[n + 1])
            for i in GROUPS[n + 1]:
                sib[i].start()
        for i in group:
            sib[i].wait_recv()
            sums[i] = part[i, c] + sib_recv[i]
            for s in range(2):
                if i == at[sides[s]]:
                    near(s).start()
        if n == 0:
            for h in range(2):
                for s in range(2):
                    farthest(s, h).start()
                for s in range(2):
                    far(s, h).start()
            project(GROUPS[1])
            for i in GROUPS[1]:
                sib[i].start()
    def owner(k):
        return ring[k % nz]

    def spread(s, h):
        n = 2 * s + h
        return remote(tok.at[z, c, h], tok.at[z, c, h], ag_s.at[n], ag_r.at[n], zdev(2 * sides[s]))

    def beside(s):
        return remote(tok.at[z, c], tok.at[z, c], ag_s.at[4 + s], ag_r.at[4 + s], zdev(sides[s]))

    def onward(s, h):
        n = 2 * s + h
        mine = tok.at[owner(-2 * sides[s]), c, h]
        return remote(mine, mine, fa_s.at[n], fa_r.at[n], zdev(sides[s]))

    def opposite(s, h):
        n = 4 + 2 * s + h
        mine = tok.at[owner(-2 * sides[s]), c, h, pl.ds(s * quarter, quarter)]
        return remote(mine, mine, fa_s.at[n], fa_r.at[n], zdev(2 * sides[s]))

    for h in range(2):
        for s in range(2):
            mine = pl.ds(s * quarter, quarter)
            far(s, h).wait_recv()
            sums[at[2 * sides[s]], h] += far_recv[s, h]
            farthest(s, h).wait_recv()
            sums[at[2 * sides[s]], h, mine] += last_recv[s, h]
            second(s, h).start()
    for s in range(2):
        near(s).wait_recv()
    for h in range(2):
        beside_sums = sums[at[0], h] + (near_recv[0, h] + near_recv[1, h])
        for s in range(2):
            second(s, h).wait_recv()
        tok[z, c, h] = beside_sums + (near_recv[2, h] + near_recv[3, h])
        for s in range(2):
            spread(s, h).start()
    for s in range(2):
        beside(s).start()

    lane = lax.broadcasted_iota(jnp.int32, (nt, LANES), 1)
    example = lax.broadcasted_iota(jnp.int32, (EXAMPLES, nt), 0)

    def share(k):
        mine = tok.at[owner(k), c]
        return remote(mine, mine, sh_s.at[k % nz], sh_r.at[k % nz], sibling)

    def accumulate(k, core):
        chip = owner(k)
        whole = tok[chip, core].reshape(nt, LANES)
        flipped = whole.T
        high = flipped[:PROJ].astype(BF16).astype(F32)
        high_ref[...] = high
        low_ref[...] = flipped[:PROJ] - high
        first = pl.multiple_of(chip * chunk + core * nt, nt)
        member = seg[:, pl.ds(first, nt)] == example
        even = jnp.where(lane < PROJ, pltpu.roll(whole, PROJ, 1), 0.0)
        odd = jnp.where(lane < PROJ, 0.0, whole)
        in_high, in_low = split(jnp.concatenate([even, odd], axis=0))
        both = jnp.concatenate([in_high, in_low], axis=1)

        def weigh(ref, p):
            pair = [
                jnp.where(member, jnp.broadcast_to(ref[pl.ds(p + parity, 1), :], member.shape), 0.0)
                for parity in range(2)
            ]
            return jnp.concatenate(pair, axis=1).astype(BF16)

        for part_of in range(2):
            ps = [8 * zz + 4 * c + 2 * jj for zz in range(4 * part_of, 4 * part_of + 4) for jj in range(2)]
            w_high = jnp.concatenate([weigh(high_ref, p) for p in ps], axis=0)
            w_low = jnp.concatenate([weigh(low_ref, p) for p in ps], axis=0)
            one = jnp.dot(w_high, both, preferred_element_type=F32)
            two = jnp.dot(w_low, in_high, preferred_element_type=F32)
            block = one[:, :LANES] + (one[:, LANES:] + two)
            xacc[pl.ds(4 * part_of, 4)] += block.reshape(4, 2 * EXAMPLES, LANES)

    def own(k):
        accumulate(k, c)

    def others(k):
        share(k).wait_recv()
        accumulate(k, 1 - c)

    share(0).start()
    own(0)
    others(0)
    for h in range(2):
        for s in range(2):
            spread(s, h).wait_recv()
            opposite(s, h).start()
            onward(s, h).start()
    for s in range(2):
        share(-2 * sides[s]).start()
    for s in range(2):
        own(-2 * sides[s])
    for s in range(2):
        beside(s).wait_recv()
        share(-sides[s]).start()
    for s in range(2):
        own(-sides[s])
    for s in range(2):
        others(-2 * sides[s])
    for s in range(2):
        others(-sides[s])
    for s in range(2):
        for h in range(2):
            onward(s, h).wait_recv()
        share(-3 * sides[s]).start()
    own(-3 * sides[0])
    for s in range(2):
        for h in range(2):
            opposite(s, h).wait_recv()
    share(4).start()
    own(-3 * sides[1])
    own(4)
    for s in range(2):
        others(-3 * sides[s])
    others(4)

    squares = xacc[...] * xacc[...]
    ss_sum[...] = jnp.sum(squares.reshape(-1, LANES), axis=0, keepdims=True)
    swap_ss = remote(ss_sum, ss_recv, ss_sem.at[0], ss_sem.at[1], sibling)
    swap_ss.start()
    message[pl.ds(0, 2 * EXAMPLES)] = xacc[z]
    pl.semaphore_wait(ready, len(line))

    home = lax.div(d, 2)
    forwards = c == lax.rem(d, 2)
    places = [lax.rem(home + m, ndp // 2) for m in range(ndp // 2)]

    def column(m):
        place = places[m]
        return remote(
            xacc.at[place], cols.at[d], col_s.at[m], col_r.at[d], (2 * place + c, t)
        )

    def column_from(source):
        return remote(xacc.at[0], cols.at[source], col_s.at[0], col_r.at[source], (source, t))

    def forward(source):
        return remote(cols.at[source], cols.at[source], fw_s.at[source], fw_r.at[source], sibling)

    sent = message.at[pl.ds(0, 2 * EXAMPLES + 1)]

    def row(k):
        return remote(
            sent, rows.at[d, pl.ds(0, 2 * EXAMPLES + 1)], row_s.at[k], row_r.at[d], (plane[k], t)
        )

    def row_from(source):
        return remote(
            sent, rows.at[source, pl.ds(0, 2 * EXAMPLES + 1)], row_s.at[1], row_r.at[source], (source, t)
        )

    for m in range(1, ndp // 2):
        column(m).start()

    @pl.when(jnp.logical_not(forwards))
    def _():
        column(0).start()

    swap_ss.wait_recv()
    message[pl.ds(2 * EXAMPLES, 1)] = ss_sum[...] + ss_recv[...]
    for k in range(1, ndp):
        row(k).start()
    rows[d, pl.ds(0, 2 * EXAMPLES + 1)] = message[pl.ds(0, 2 * EXAMPLES + 1)]

    def matrix(ref, jj):
        return ref[:, pl.ds(jj * EXAMPLES, EXAMPLES), :].reshape(ndp * EXAMPLES, LANES)

    def place_columns():
        for jj in range(2):
            right_ref[:, pl.ds(jj * LANES, LANES)] = matrix(cols, jj)

    @pl.when(forwards)
    def _():
        cols[d] = xacc[home]
        forward(d).start()
        for k in range(1, ndp):
            source = plane[k]
            column_from(source).wait_recv()
            forward(source).start()
        place_columns()

    for k in range(1, ndp):
        row_from(plane[k]).wait_recv()
    trace = jnp.sum(rows[:, pl.ds(2 * EXAMPLES, 1), :], axis=0)
    trace = jnp.sum(trace, axis=1, keepdims=True)
    scale = 1.0 / (trace / (PROJ * PROJ) + 1e-6)
    for jj in range(2):
        left_ref[:, pl.ds(jj * LANES, LANES)] = matrix(rows, jj) * scale

    @pl.when(jnp.logical_not(forwards))
    def _():
        for k in range(ndp):
            forward(plane[k]).wait_recv()
        place_columns()

    for copy in sib + [swap_ss] + [share(k) for k in range(nz)]:
        copy.wait_send()
    for s in range(2):
        for copy in (near(s), beside(s)):
            copy.wait_send()
        for h in range(2):
            for copy in (
                far(s, h), farthest(s, h), second(s, h), spread(s, h), onward(s, h), opposite(s, h)
            ):
                copy.wait_send()
    for m in range(1, ndp // 2):
        column(m).wait_send()
    for k in range(1, ndp):
        row(k).wait_send()

    @pl.when(forwards)
    def _():
        for k in range(ndp):
            forward(k).wait_send()

    @pl.when(jnp.logical_not(forwards))
    def _():
        column(0).wait_send()


def shards(ndp, nz, grad_up, activations, segment_ids, proj_out, proj_in):
    tokens, hidden = grad_up.shape
    features = activations.shape[1]
    nt = tokens // (2 * nz)
    rows = 2 * EXAMPLES
    block = 4 * PROJ
    dma = pltpu.SemaphoreType.DMA
    halves = (2, nt // 2, LANES)
    arrays = (grad_up, activations, segment_ids, proj_out, proj_in)
    in_hbm = [pltpu.with_memory_space_constraint(array, pltpu.HBM) for array in arrays]
    left, right = pl.pallas_call(
        functools.partial(kernel, ndp, nz, nt),
        out_shape=[
            jax.ShapeDtypeStruct((ndp * EXAMPLES, block), F32),
            jax.ShapeDtypeStruct((ndp * EXAMPLES, block), F32),
        ],
        in_specs=[pl.BlockSpec(memory_space=pltpu.HBM)] * 5,
        out_specs=[pl.BlockSpec(memory_space=pltpu.VMEM)] * 2,
        scratch_shapes=[
            pltpu.VMEM((nz, 2 * nt, hidden), BF16),
            pltpu.VMEM((nz, 2 * nt, features), BF16),
            pltpu.VMEM((1, tokens), jnp.int32),
            pltpu.VMEM((2 * PROJ, hidden), BF16),
            pltpu.VMEM((2 * PROJ, features), BF16),
            pltpu.VMEM((hidden, 2 * PROJ), BF16),
            pltpu.VMEM((features, 2 * PROJ), BF16),
            pltpu.VMEM((nz, 2) + halves, F32),
            pltpu.VMEM((nz,) + halves, F32),
            pltpu.VMEM((nz,) + halves, F32),
            pltpu.VMEM((2,) + halves, F32),
            pltpu.VMEM((2, 2, nt // 4, LANES), F32),
            pltpu.VMEM((4,) + halves, F32),
            pltpu.VMEM((nz, 2) + halves, F32),
            pltpu.VMEM((PROJ, nt), F32),
            pltpu.VMEM((PROJ, nt), F32),
            pltpu.VMEM((nz, rows, LANES), F32),
            pltpu.VMEM((rows + 8, LANES), F32),
            pltpu.VMEM((ndp, rows + 8, LANES), F32),
            pltpu.VMEM((ndp, rows, LANES), F32),
            pltpu.VMEM((1, LANES), F32),
            pltpu.VMEM((1, LANES), F32),
            dma((nz,)), dma((nz,)), dma((3,)),
            dma((nz,)), dma((nz,)), dma((8,)), dma((8,)), dma((6,)), dma((6,)),
            dma((6,)), dma((6,)), dma((8,)), dma((8,)), dma((nz,)), dma((nz,)),
            dma((ndp,)), dma((ndp,)), dma((ndp,)), dma((ndp,)), dma((ndp,)), dma((ndp,)),
            dma((2,)), pltpu.SemaphoreType.REGULAR,
        ],
        compiler_params=pltpu.CompilerParams(
            collective_id=0, has_side_effects=True, vmem_limit_bytes=24 * 2**20
        ),
        cost_estimate=pl.CostEstimate(
            flops=2 * tokens * (hidden + features) * PROJ,
            bytes_accessed=2 * tokens * (hidden + features),
            transcendentals=0,
        ),
    )(*in_hbm)
    return lax.dot_general(
        left, right, (((0,), (0,)), ((), ())),
        precision=lax.Precision.HIGH, preferred_element_type=F32,
    )


def solution(mesh):
    in_specs = (
        P("dp", "tensor"),
        P("dp", "tensor"),
        P("dp", None),
        P(None, "tensor"),
        P(None, "tensor"),
    )
    body = functools.partial(shards, mesh.shape["dp"], mesh.shape["tensor"] // 2)
    return jax.shard_map(
        body, mesh=mesh, in_specs=in_specs, out_specs=P("tensor", "dp"), check_vma=False
    )
```

```python
import functools

import jax
import jax.numpy as jnp
from jax import lax
from jax.experimental import pallas as pl
from jax.experimental.pallas import tpu as pltpu
from jax.sharding import PartitionSpec as P

MESH = pl.DeviceIdType.MESH
F32 = jnp.float32
BF16 = jnp.bfloat16
EXAMPLES = 16
PROJ = 64
LANES = 128
DEPTH = 256
SIDE = 4


def split(x):
    high = x.astype(BF16)
    low = (x - high.astype(F32)).astype(BF16)
    return high, low


ORDER = (4, 3, -3, 1, -1, 2, -2, 0)
GROUPS = ((0, 1, 2), (3, 4), (5, 6), (7,))


def kernel(
    ndp, nz, nt,
    grad_hbm, act_hbm, seg_hbm, po_hbm, pi_hbm, left_ref, right_ref,
    gbuf, abuf, seg, wout, win, wt_out, wt_in, part, sib_recv, sums, far_recv, last_recv, near_recv, tok,
    high_ref, low_ref, xacc, message, rows, cols, ss_sum, ss_recv,
    g_sem, a_sem, w_sem, sib_s, sib_r, far_s, far_r, near_s, near_r, ag_s, ag_r, fa_s, fa_r,
    sh_s, sh_r, row_s, row_r, col_s, col_r, fw_s, fw_r, ss_sem, ready,
):
    d = lax.axis_index("dp")
    t = lax.axis_index("tensor")
    z, c = lax.div(t, 2), lax.rem(t, 2)
    ring = [lax.rem(z + k, nz) for k in range(nz)]
    plane = [lax.rem(d + k, ndp) for k in range(ndp)]
    sibling = (d, t + 1 - 2 * c)
    chunk = 2 * nt

    def zdev(k):
        return (d, ring[k % nz] * 2 + c)

    def remote(src, dst, send, recv, device):
        return pltpu.make_async_remote_copy(
            src_ref=src, dst_ref=dst, send_sem=send, recv_sem=recv,
            device_id=device, device_id_type=MESH,
        )

    barrier = pltpu.get_barrier_semaphore()
    line = [(lax.div(d, SIDE) * SIDE + lax.rem(d + k, SIDE), t) for k in range(1, SIDE)]
    column_peers = [(plane[SIDE * k], t) for k in range(1, ndp // SIDE)]
    greeted = [zdev(k) for k in (1, -1, 2, -2)] + line + column_peers + [sibling]
    for device in greeted:
        pl.semaphore_signal(barrier, inc=1, device_id=device, device_id_type=MESH)

    weights = [
        pltpu.make_async_copy(po_hbm, wout.at[pl.ds(0, PROJ)], w_sem.at[0]),
        pltpu.make_async_copy(pi_hbm, win.at[pl.ds(PROJ, PROJ)], w_sem.at[1]),
        pltpu.make_async_copy(seg_hbm, seg, w_sem.at[2]),
    ]
    for copy in weights:
        copy.start()
    loads = []
    for i in range(nz):
        first = pl.multiple_of(ring[ORDER[i] % nz] * chunk, chunk)
        loads.append((
            pltpu.make_async_copy(grad_hbm.at[pl.ds(first, chunk)], gbuf.at[i], g_sem.at[i]),
            pltpu.make_async_copy(act_hbm.at[pl.ds(first, chunk)], abuf.at[i], a_sem.at[i]),
        ))
    for i in GROUPS[0]:
        loads[i][0].start()
        loads[i][1].start()

    wout[pl.ds(PROJ, PROJ)] = jnp.zeros((PROJ, wout.shape[1]), BF16)
    win[pl.ds(0, PROJ)] = jnp.zeros((PROJ, win.shape[1]), BF16)
    xacc[...] = jnp.zeros_like(xacc)
    for copy in weights:
        copy.wait()
    wt_out[...] = wout[...].T
    wt_in[...] = win[...].T

    def project(group):
        for i in group:
            loads[i][0].wait()
            loads[i][1].wait()
        if group == GROUPS[0]:
            for i in range(len(group), nz):
                loads[i][0].start()
                loads[i][1].start()
        total = {}
        for source, weight in ((gbuf, wt_out), (abuf, wt_in)):
            for first in range(0, weight.shape[0], DEPTH):
                for i in group:
                    term = jnp.dot(
                        source[i, :, pl.ds(first, DEPTH)], weight[pl.ds(first, DEPTH)],
                        preferred_element_type=F32,
                    )
                    total[i] = total[i] + term if i in total else term
        for i in group:
            part[i] = total[i].reshape((2, 2, nt // 2, LANES))

    project(GROUPS[0])
    pl.semaphore_wait(barrier, len(greeted))
    for device in line:
        pl.semaphore_signal(ready, inc=1, device_id=device, device_id_type=MESH)

    sib = [
        remote(part.at[i, 1 - c], sib_recv.at[i], sib_s.at[i], sib_r.at[i], sibling)
        for i in range(nz)
    ]
    at = {offset: i for i, offset in enumerate(ORDER)}
    sides = (1, -1)
    quarter = nt // 4

    def far(s, h):
        n = 2 * s + h
        return remote(
            sums.at[at[3 * sides[s]], h], far_recv.at[s, h], far_s.at[n], far_r.at[n], zdev(sides[s])
        )

    def farthest(s, h):
        n = 4 + 2 * s + h
        return remote(
            sums.at[at[4], h, pl.ds(s * quarter, quarter)], last_recv.at[s, h], far_s.at[n], far_r.at[n],
            zdev(2 * sides[s]),
        )

    def near(s):
        return remote(sums.at[at[sides[s]]], near_recv.at[s], near_s.at[s], near_r.at[s], zdev(sides[s]))

    def second(s, h):
        n = 2 + 2 * s + h
        return remote(
            sums.at[at[2 * sides[s]], h], near_recv.at[2 + s, h], near_s.at[n], near_r.at[n],
            zdev(2 * sides[s]),
        )

    for i in GROUPS[0]:
        sib[i].start()
    for n, group in enumerate(GROUPS):
        if 0 < n < len(GROUPS) - 1:
            project(GROUPS[n + 1])
            for i in GROUPS[n + 1]:
                sib[i].start()
        for i in group:
            sib[i].wait_recv()
            sums[i] = part[i, c] + sib_recv[i]
            for s in range(2):
                if i == at[sides[s]]:
                    near(s).start()
        if n == 0:
            for h in range(2):
                for s in range(2):
                    farthest(s, h).start()
                for s in range(2):
                    far(s, h).start()
            project(GROUPS[1])
            for i in GROUPS[1]:
                sib[i].start()
    def owner(k):
        return ring[k % nz]

    def spread(s, h):
        n = 2 * s + h
        return remote(tok.at[z, c, h], tok.at[z, c, h], ag_s.at[n], ag_r.at[n], zdev(2 * sides[s]))

    def beside(s):
        return remote(tok.at[z, c], tok.at[z, c], ag_s.at[4 + s], ag_r.at[4 + s], zdev(sides[s]))

    def onward(s, h):
        n = 2 * s + h
        mine = tok.at[owner(-2 * sides[s]), c, h]
        return remote(mine, mine, fa_s.at[n], fa_r.at[n], zdev(sides[s]))

    def opposite(s, h):
        n = 4 + 2 * s + h
        mine = tok.at[owner(-2 * sides[s]), c, h, pl.ds(s * quarter, quarter)]
        return remote(mine, mine, fa_s.at[n], fa_r.at[n], zdev(2 * sides[s]))

    for h in range(2):
        for s in range(2):
            mine = pl.ds(s * quarter, quarter)
            far(s, h).wait_recv()
            sums[at[2 * sides[s]], h] += far_recv[s, h]
            farthest(s, h).wait_recv()
            sums[at[2 * sides[s]], h, mine] += last_recv[s, h]
            second(s, h).start()
    for s in range(2):
        near(s).wait_recv()
    for h in range(2):
        beside_sums = sums[at[0], h] + (near_recv[0, h] + near_recv[1, h])
        for s in range(2):
            second(s, h).wait_recv()
        tok[z, c, h] = beside_sums + (near_recv[2, h] + near_recv[3, h])
        for s in range(2):
            spread(s, h).start()
    for s in range(2):
        beside(s).start()

    lane = lax.broadcasted_iota(jnp.int32, (nt, LANES), 1)
    example = lax.broadcasted_iota(jnp.int32, (EXAMPLES, nt), 0)

    def share(k):
        mine = tok.at[owner(k), c]
        return remote(mine, mine, sh_s.at[k % nz], sh_r.at[k % nz], sibling)

    def accumulate(k, core):
        chip = owner(k)
        whole = tok[chip, core].reshape(nt, LANES)
        flipped = whole.T
        high = flipped[:PROJ].astype(BF16).astype(F32)
        high_ref[...] = high
        low_ref[...] = flipped[:PROJ] - high
        first = pl.multiple_of(chip * chunk + core * nt, nt)
        member = seg[:, pl.ds(first, nt)] == example
        even = jnp.where(lane < PROJ, pltpu.roll(whole, PROJ, 1), 0.0)
        odd = jnp.where(lane < PROJ, 0.0, whole)
        in_high, in_low = split(jnp.concatenate([even, odd], axis=0))
        both = jnp.concatenate([in_high, in_low], axis=1)

        def weigh(ref, p):
            pair = [
                jnp.where(member, jnp.broadcast_to(ref[pl.ds(p + parity, 1), :], member.shape), 0.0)
                for parity in range(2)
            ]
            return jnp.concatenate(pair, axis=1).astype(BF16)

        for part_of in range(2):
            ps = [8 * zz + 4 * c + 2 * jj for zz in range(4 * part_of, 4 * part_of + 4) for jj in range(2)]
            w_high = jnp.concatenate([weigh(high_ref, p) for p in ps], axis=0)
            w_low = jnp.concatenate([weigh(low_ref, p) for p in ps], axis=0)
            one = jnp.dot(w_high, both, preferred_element_type=F32)
            two = jnp.dot(w_low, in_high, preferred_element_type=F32)
            block = one[:, :LANES] + (one[:, LANES:] + two)
            xacc[pl.ds(4 * part_of, 4)] += block.reshape(4, 2 * EXAMPLES, LANES)

    def own(k):
        accumulate(k, c)

    def others(k):
        share(k).wait_recv()
        accumulate(k, 1 - c)

    share(0).start()
    own(0)
    others(0)
    for h in range(2):
        for s in range(2):
            spread(s, h).wait_recv()
            onward(s, h).start()
            opposite(s, h).start()
    for s in range(2):
        share(-2 * sides[s]).start()
    for s in range(2):
        own(-2 * sides[s])
    for s in range(2):
        beside(s).wait_recv()
        share(-sides[s]).start()
    for s in range(2):
        own(-sides[s])
    for s in range(2):
        others(-2 * sides[s])
    for s in range(2):
        others(-sides[s])
    for s in range(2):
        for h in range(2):
            onward(s, h).wait_recv()
        share(-3 * sides[s]).start()
    own(-3 * sides[0])
    for s in range(2):
        for h in range(2):
            opposite(s, h).wait_recv()
    share(4).start()
    own(-3 * sides[1])
    own(4)
    for s in range(2):
        others(-3 * sides[s])
    others(4)

    squares = xacc[...] * xacc[...]
    ss_sum[...] = jnp.sum(squares.reshape(-1, LANES), axis=0, keepdims=True)
    swap_ss = remote(ss_sum, ss_recv, ss_sem.at[0], ss_sem.at[1], sibling)
    swap_ss.start()
    message[pl.ds(0, 2 * EXAMPLES)] = xacc[z]
    pl.semaphore_wait(ready, len(line))

    home = lax.div(d, 2)
    forwards = c == lax.rem(d, 2)
    places = [lax.rem(home + m, ndp // 2) for m in range(ndp // 2)]

    def column(m):
        place = places[m]
        return remote(
            xacc.at[place], cols.at[d], col_s.at[m], col_r.at[d], (2 * place + c, t)
        )

    def column_from(source):
        return remote(xacc.at[0], cols.at[source], col_s.at[0], col_r.at[source], (source, t))

    def forward(source):
        return remote(cols.at[source], cols.at[source], fw_s.at[source], fw_r.at[source], sibling)

    sent = message.at[pl.ds(0, 2 * EXAMPLES + 1)]

    def row(k):
        return remote(
            sent, rows.at[d, pl.ds(0, 2 * EXAMPLES + 1)], row_s.at[k], row_r.at[d], (plane[k], t)
        )

    def row_from(source):
        return remote(
            sent, rows.at[source, pl.ds(0, 2 * EXAMPLES + 1)], row_s.at[1], row_r.at[source], (source, t)
        )

    for m in range(1, ndp // 2):
        column(m).start()

    @pl.when(jnp.logical_not(forwards))
    def _():
        column(0).start()

    swap_ss.wait_recv()
    message[pl.ds(2 * EXAMPLES, 1)] = ss_sum[...] + ss_recv[...]
    for k in range(1, ndp):
        row(k).start()
    rows[d, pl.ds(0, 2 * EXAMPLES + 1)] = message[pl.ds(0, 2 * EXAMPLES + 1)]

    def matrix(ref, jj):
        return ref[:, pl.ds(jj * EXAMPLES, EXAMPLES), :].reshape(ndp * EXAMPLES, LANES)

    def place_columns():
        for jj in range(2):
            right_ref[:, pl.ds(jj * LANES, LANES)] = matrix(cols, jj)

    @pl.when(forwards)
    def _():
        cols[d] = xacc[home]
        forward(d).start()
        for k in range(1, ndp):
            source = plane[k]
            column_from(source).wait_recv()
            forward(source).start()
        place_columns()

    for k in range(1, ndp):
        row_from(plane[k]).wait_recv()
    trace = jnp.sum(rows[:, pl.ds(2 * EXAMPLES, 1), :], axis=0)
    trace = jnp.sum(trace, axis=1, keepdims=True)
    scale = 1.0 / (trace / (PROJ * PROJ) + 1e-6)
    for jj in range(2):
        left_ref[:, pl.ds(jj * LANES, LANES)] = matrix(rows, jj) * scale

    @pl.when(jnp.logical_not(forwards))
    def _():
        for k in range(ndp):
            forward(plane[k]).wait_recv()
        place_columns()

    for copy in sib + [swap_ss] + [share(k) for k in range(nz)]:
        copy.wait_send()
    for s in range(2):
        for copy in (near(s), beside(s)):
            copy.wait_send()
        for h in range(2):
            for copy in (
                far(s, h), farthest(s, h), second(s, h), spread(s, h), onward(s, h), opposite(s, h)
            ):
                copy.wait_send()
    for m in range(1, ndp // 2):
        column(m).wait_send()
    for k in range(1, ndp):
        row(k).wait_send()

    @pl.when(forwards)
    def _():
        for k in range(ndp):
            forward(k).wait_send()

    @pl.when(jnp.logical_not(forwards))
    def _():
        column(0).wait_send()


def shards(ndp, nz, grad_up, activations, segment_ids, proj_out, proj_in):
    tokens, hidden = grad_up.shape
    features = activations.shape[1]
    nt = tokens // (2 * nz)
    rows = 2 * EXAMPLES
    block = 4 * PROJ
    dma = pltpu.SemaphoreType.DMA
    halves = (2, nt // 2, LANES)
    arrays = (grad_up, activations, segment_ids, proj_out, proj_in)
    in_hbm = [pltpu.with_memory_space_constraint(array, pltpu.HBM) for array in arrays]
    left, right = pl.pallas_call(
        functools.partial(kernel, ndp, nz, nt),
        out_shape=[
            jax.ShapeDtypeStruct((ndp * EXAMPLES, block), F32),
            jax.ShapeDtypeStruct((ndp * EXAMPLES, block), F32),
        ],
        in_specs=[pl.BlockSpec(memory_space=pltpu.HBM)] * 5,
        out_specs=[pl.BlockSpec(memory_space=pltpu.VMEM)] * 2,
        scratch_shapes=[
            pltpu.VMEM((nz, 2 * nt, hidden), BF16),
            pltpu.VMEM((nz, 2 * nt, features), BF16),
            pltpu.VMEM((1, tokens), jnp.int32),
            pltpu.VMEM((2 * PROJ, hidden), BF16),
            pltpu.VMEM((2 * PROJ, features), BF16),
            pltpu.VMEM((hidden, 2 * PROJ), BF16),
            pltpu.VMEM((features, 2 * PROJ), BF16),
            pltpu.VMEM((nz, 2) + halves, F32),
            pltpu.VMEM((nz,) + halves, F32),
            pltpu.VMEM((nz,) + halves, F32),
            pltpu.VMEM((2,) + halves, F32),
            pltpu.VMEM((2, 2, nt // 4, LANES), F32),
            pltpu.VMEM((4,) + halves, F32),
            pltpu.VMEM((nz, 2) + halves, F32),
            pltpu.VMEM((PROJ, nt), F32),
            pltpu.VMEM((PROJ, nt), F32),
            pltpu.VMEM((nz, rows, LANES), F32),
            pltpu.VMEM((rows + 8, LANES), F32),
            pltpu.VMEM((ndp, rows + 8, LANES), F32),
            pltpu.VMEM((ndp, rows, LANES), F32),
            pltpu.VMEM((1, LANES), F32),
            pltpu.VMEM((1, LANES), F32),
            dma((nz,)), dma((nz,)), dma((3,)),
            dma((nz,)), dma((nz,)), dma((8,)), dma((8,)), dma((6,)), dma((6,)),
            dma((6,)), dma((6,)), dma((8,)), dma((8,)), dma((nz,)), dma((nz,)),
            dma((ndp,)), dma((ndp,)), dma((ndp,)), dma((ndp,)), dma((ndp,)), dma((ndp,)),
            dma((2,)), pltpu.SemaphoreType.REGULAR,
        ],
        compiler_params=pltpu.CompilerParams(
            collective_id=0, has_side_effects=True, vmem_limit_bytes=24 * 2**20
        ),
        cost_estimate=pl.CostEstimate(
            flops=2 * tokens * (hidden + features) * PROJ,
            bytes_accessed=2 * tokens * (hidden + features),
            transcendentals=0,
        ),
    )(*in_hbm)
    return lax.dot_general(
        left, right, (((0,), (0,)), ((), ())),
        precision=lax.Precision.HIGH, preferred_element_type=F32,
    )


def solution(mesh):
    in_specs = (
        P("dp", "tensor"),
        P("dp", "tensor"),
        P("dp", None),
        P(None, "tensor"),
        P(None, "tensor"),
    )
    body = functools.partial(shards, mesh.shape["dp"], mesh.shape["tensor"] // 2)
    return jax.shard_map(
        body, mesh=mesh, in_specs=in_specs, out_specs=P("tensor", "dp"), check_vma=False
    )
```
